256 devices in a mesh: dp: 4 (over x), seq: 64 (over z, y, core).
Axes of the slice: x: 4, y: 4, z: 8, core: 2. Of those that a mesh axis runs over, the one named last changes fastest.
Arguments:
- hidden: bfloat16 [8, 16384, 4096], P('dp', 'seq'), may hold values from -6 to 6
- doc_lengths: int32 [8, 8], P('dp'), may hold values from 1 to 4096, 16384 in all within a row
- partner: int32 [64], replicated, may hold values from 0 to 63, as said below
- closing_layer_weight: float32 [4096], replicated, may hold values from 0.25 to 1.75
Outputs:
- hidden_grad: bfloat16 [8, 16384, 4096], P('dp', 'seq')
- loss_value: float32 [], replicated
The draws below stay inside these ranges and needn't reach their ends.
Inputs may be any that keep to these rules, and one draw needn't show every extreme that they name: partner pairs the documents: partner[partner[i]] = i and partner[i] != i.
All inputs are finite; a program needn't handle non-finite values.
Results may differ from the reference program's by a relative error of at most 0.005.
Values sent between devices are 32-bit elements; how exact they have to be, the bound alone decides.
A program may use at most 64 MiB of HBM per device.

```python
import math
import jax
import jax.numpy as jnp
import numpy as np
from jax import lax

D = 4096
DOCS_ROW = 8
ROWS = 8
LEN = 16384
NDOC = 64
MOST = 4096


def draw_partner(key, part):
    key = jax.random.fold_in(key, 7)
    order = jax.random.permutation(key, NDOC).astype(jnp.int32)
    paired = order.reshape(NDOC // 2, 2)[:, ::-1].reshape(-1)
    return jnp.zeros((NDOC,), jnp.int32).at[order].set(paired)


def levels(own_key, dims, pieces, least, largest):
    def one(position, shards_of):
        steps = jax.random.uniform(jax.random.fold_in(jax.random.fold_in(own_key, 6), position), (shards_of,), jnp.float32, least / len(pieces), largest / len(pieces))
        return jnp.repeat(jnp.exp(steps), dims[position] // shards_of).reshape((-1,) + (1,) * (len(dims) - position - 1))

    loudness = one(*pieces[0])
    for cut in pieces[1:]:
        loudness = loudness * one(*cut)
    return loudness


def length_profile(count, total, bound, slope):
    loads = [(1 << 20) // math.isqrt(rank ** slope) + 1 for rank in range(2, count + 1)]
    surplus, counts = total - bound - (count - 1), [1] * (count - 1)
    while surplus > 0:
        free = [i for i in range(count - 1) if counts[i] < bound]
        mass, remaining = sum([loads[i] for i in free]), surplus
        for i in free:
            more = min(bound - counts[i], max(1, remaining * loads[i] // mass), surplus)
            counts[i] = counts[i] + more
            surplus = surplus - more
    return np.array([bound] + counts)


def uneven(own_key, count, total, most, slope):
    if count == 2:
        one = jax.random.randint(own_key, (), max(1, total - most), min(most, total - 1) + 1)
        return jnp.stack([one, total - one])
    sizes = jnp.asarray(length_profile(count, total, most, slope), jnp.int32)
    couples = (count - 1) // 2
    giver, taker = sizes[1:1 + 2 * couples:2], sizes[2:2 + 2 * couples:2]
    margin = jnp.minimum(giver - 1, most - taker)
    passed = jax.random.randint(jax.random.fold_in(own_key, 1), (couples,), 0, 1 << 20) % (margin + 1)
    sizes = sizes.at[1:1 + 2 * couples:2].set(giver - passed).at[2:2 + 2 * couples:2].set(taker + passed)
    return sizes[jax.random.permutation(jax.random.fold_in(own_key, 2), count)]


def normal_values(own_key, shape, spread, limit, shards=(), held_as=jnp.bfloat16):
    level = levels(own_key, shape, shards, -0.22, 0.18) if shards else 1.0
    array = jax.random.normal(own_key, shape, jnp.float32) * spread * level
    return jnp.minimum(jnp.maximum(array, -limit), limit).astype(held_as)


def setup_inputs(seed: int = 0) -> dict:
    splits = jax.random.split(jax.random.key(seed), 5)
    return {
        "hidden": normal_values(splits[0], (ROWS, LEN, D), 1.0, 6.0, ((0, 4), (1, 64))),
        "doc_lengths": jax.vmap(lambda own: uneven(own, DOCS_ROW, LEN, MOST, 2))(jax.random.split(splits[1], ROWS)).reshape((ROWS, DOCS_ROW)).astype(jnp.int32),
        "partner": draw_partner(jax.random.fold_in(splits[4], 71), 0),
        "closing_layer_weight": jnp.clip(1.0 + 0.15 * jax.random.normal(splits[3], (D,), jnp.float32), 0.25, 1.75),
    }


sharpness_divisor = 0.05
derivative_multiplier = 524288.0

def contrast(cosine_table, partner):
    count_docs = cosine_table.shape[0]
    embedding_lengths = jnp.sqrt(jnp.diagonal(cosine_table) + 1e-06)
    unnormalized_pair_affinity = cosine_table / (embedding_lengths[:, None] * embedding_lengths[None, :]) / sharpness_divisor
    rows_idx = jnp.arange(count_docs, dtype=jnp.int32)
    identity_selector = rows_idx[:, None] == rows_idx[None, :]
    weights = jnp.where(identity_selector, jnp.float32(0.0), jnp.exp(unnormalized_pair_affinity))
    log_total = jnp.log(lax.optimization_barrier(jnp.sum(weights, axis=1)))
    target = lax.optimization_barrier(jnp.sum(jnp.where(rows_idx[None, :] == partner[:, None], unnormalized_pair_affinity, jnp.float32(0.0)), axis=1))
    return jnp.mean(log_total - target)

def membership(lengths, positions):
    finish = jnp.cumsum(lengths)
    starts = finish - lengths
    return (positions[None, :] >= starts[:, None]) & (positions[None, :] < finish[:, None])

def reference(hidden, doc_lengths, partner, closing_layer_weight):
    positions = jnp.arange(LEN, dtype=jnp.int32)

    def pool_row(items):
        concatenated_token_hidden, lengths = items
        float_values = concatenated_token_hidden.astype(jnp.float32)
        inv_rms = lax.rsqrt(lax.optimization_barrier(jnp.mean(float_values * float_values, axis=-1, keepdims=True)) + 1e-06)
        normed = (float_values * inv_rms * closing_layer_weight).astype(jnp.bfloat16)
        member = membership(lengths, positions).astype(jnp.bfloat16)
        sums = jnp.dot(member, normed, preferred_element_type=jnp.float32)
        return sums / lengths.astype(jnp.float32)[:, None]
    mean_pooled = lax.map(pool_row, (hidden, doc_lengths)).reshape(NDOC, D)
    cosine_table = jnp.dot(mean_pooled, mean_pooled.T, precision=lax.Precision.HIGHEST)
    loss_value, back = jax.vjp(lambda matrix: contrast(matrix, partner), cosine_table)
    grad_gram = back(jnp.float32(1.0))[0]
    grad_pooled = jnp.dot(grad_gram + grad_gram.T, mean_pooled, precision=lax.Precision.HIGHEST)
    scaled = grad_pooled.reshape(ROWS, DOCS_ROW, D) * (derivative_multiplier / doc_lengths.astype(jnp.float32))[:, :, None]

    def back_row(items):
        concatenated_token_hidden, lengths, row_scaled = items
        float_values = concatenated_token_hidden.astype(jnp.float32)
        inv_rms = lax.rsqrt(lax.optimization_barrier(jnp.mean(float_values * float_values, axis=-1, keepdims=True)) + 1e-06)
        member = membership(lengths, positions).astype(jnp.float32)
        grad_normed = jnp.dot(member.T, row_scaled, precision=lax.Precision.HIGHEST)
        weighted = closing_layer_weight * grad_normed
        inner = lax.optimization_barrier(jnp.mean(float_values * weighted, axis=-1, keepdims=True))
        return (inv_rms * weighted - float_values * inv_rms ** 3 * inner).astype(jnp.bfloat16)
    hidden_grad = lax.map(back_row, (hidden, doc_lengths, scaled))
    return (hidden_grad, loss_value)
```

```python
import jax
import jax.numpy as jnp
from jax import lax
from jax.experimental import pallas as pl
from jax.experimental.pallas import tpu as pltpu
from jax.sharding import PartitionSpec as P

MESH = pl.DeviceIdType.MESH
F32, BF16 = jnp.float32, jnp.bfloat16

SHARPNESS = 0.05
LOSS_SCALE = 524288.0
EPS = 1e-06

NX, NZ, NY, NCORE = 4, 8, 4, 2
CHIPS = NZ * NY
PLANE = NX * NY
D = 4096
DOCS_ROW = 8
NDOC = 64
TOK = 256
LANES = D // CHIPS
ZCOLS = LANES * NY
PARTS = 4
NEAR_FIRST = (0, 1, 7, 2, 6, 3, 5, 4)


def bounds(len_ref, row):
    along = len_ref[pl.ds(row, 1), :].astype(F32)
    k = lax.broadcasted_iota(jnp.int32, (DOCS_ROW, DOCS_ROW), 0)
    l = lax.broadcasted_iota(jnp.int32, (DOCS_ROW, DOCS_ROW), 1)
    spread = jnp.broadcast_to(along, (DOCS_ROW, DOCS_ROW))
    down = jnp.sum(jnp.where(k == l, spread, 0.0), axis=1, keepdims=True)
    finish_down = jnp.sum(jnp.where(l <= k, spread, 0.0), axis=1, keepdims=True)
    start_down = finish_down - down
    start_along = jnp.sum(jnp.where(k < l, jnp.broadcast_to(down, (DOCS_ROW, DOCS_ROW)), 0.0), axis=0, keepdims=True)
    return down, start_down, finish_down, start_along


def split(value):
    high = value.astype(BF16)
    return high, (value - high.astype(F32)).astype(BF16)


def nt_dot(a, b):
    return lax.dot_general(a, b, (((1,), (1,)), ((), ())), preferred_element_type=F32)


def pool_kernel(
    h_ref, len_ref, partner_ref, w_ref,
    bb_ref, a_ref, ww_ref, loss_ref,
    hv, sb, csend, crecv, rbuf, rs_in, pooled, u, gram, sym,
    load_sem, core_send, core_recv, rs_send, rs_recv, z_send, z_recv, p_send, p_recv, f_send, f_recv,
):
    x = lax.axis_index("dp")
    seq = lax.axis_index("seq")
    chip = lax.div(seq, NCORE)
    core = lax.rem(seq, NCORE)
    z = lax.div(chip, NY)
    y = lax.rem(chip, NY)
    rows = (1 - core, core)

    def device(to_x, to_chip):
        return (to_x, to_chip * NCORE + core)

    def plane_peer(i):
        q = lax.rem(x * NY + y + i, PLANE)
        return device(lax.div(q, NY), z * NY + lax.rem(q, NY))

    other_core = (x, chip * NCORE + 1 - core)

    loads = []
    for o in range(2):
        for q in range(PARTS):
            part = pl.ds(q * (TOK // PARTS), TOK // PARTS)
            copy = pltpu.make_async_copy(
                h_ref.at[rows[o], part], hv.at[o, part], load_sem.at[o * PARTS + q]
            )
            copy.start()
            loads.append(copy)

    barrier = pltpu.get_barrier_semaphore()

    def hello(i, _):
        to = device(x, lax.rem(chip + i, CHIPS))
        pl.semaphore_signal(barrier, inc=1, device_id=to, device_id_type=MESH)
        return 0

    def hello_plane(i, _):
        to = device(lax.rem(x + 1 + lax.div(i, NY), NX), z * NY + lax.rem(y + i, NY))
        pl.semaphore_signal(barrier, inc=1, device_id=to, device_id_type=MESH)
        return 0

    lax.fori_loop(1, CHIPS, hello, 0)
    lax.fori_loop(0, (NX - 1) * NY, hello_plane, 0)
    pl.semaphore_signal(barrier, inc=1, device_id=other_core, device_id_type=MESH)

    def squares(o, q):
        def step(n, _):
            at = pl.ds(pl.multiple_of(q * (TOK // PARTS) + n * 32, 32), 32)
            acc = jnp.zeros((32, 128), F32)
            for t in range(D // 128):
                v = hv[o, at, t * 128 : (t + 1) * 128].astype(F32)
                acc = acc + v * v
            total = jnp.sum(acc, axis=1, keepdims=True)
            sb[o, at, :] = jnp.broadcast_to(lax.rsqrt(total * (1.0 / D) + EPS), (32, 128))
            return 0

        lax.fori_loop(0, TOK // PARTS // 32, step, 0)

    along = (seq * TOK + lax.broadcasted_iota(jnp.int32, (DOCS_ROW, TOK), 1)).astype(F32)

    def selector(o):
        _, start_down, finish_down, _ = bounds(len_ref, rows[o])
        inv = sb[o].T[0:DOCS_ROW, :]
        member = (along >= start_down) & (along < finish_down)
        high, low = split(jnp.where(member, inv, 0.0))
        return jnp.concatenate([high, low], axis=0)

    def sums(chosen, o, q):
        both = jnp.dot(
            chosen, hv[o, :, q * (D // PARTS) : (q + 1) * (D // PARTS)], preferred_element_type=F32
        )
        return both[0:DOCS_ROW] + both[DOCS_ROW : 2 * DOCS_ROW]

    per_part = CHIPS // PARTS
    for q in range(PARTS):
        loads[q].wait()
        squares(0, q)
    chosen = selector(0)
    core_copies = []
    for q in range(PARTS):
        part = sums(chosen, 0, q)
        for b in range(per_part):
            csend[q * per_part + b] = part[:, b * LANES : (b + 1) * LANES]
        if q == 0:
            pl.semaphore_wait(barrier, CHIPS - 1 + (NX - 1) * NY + 1)
        at = pl.ds(q * per_part, per_part)
        copy = pltpu.make_async_remote_copy(
            csend.at[at], crecv.at[at], core_send.at[q], core_recv.at[q],
            device_id=other_core, device_id_type=MESH,
        )
        copy.start()
        core_copies.append(copy)
    for q in range(PARTS):
        loads[PARTS + q].wait()
        squares(1, q)
    chosen = selector(1)
    for q in range(PARTS):
        part = sums(chosen, 1, q)
        core_copies[q].wait()
        for b in range(per_part):
            rbuf[q * per_part + b] = part[:, b * LANES : (b + 1) * LANES] + crecv[q * per_part + b]

        def scatter(b, _):
            @pl.when(b != chip)
            def _():
                pltpu.make_async_remote_copy(
                    rbuf.at[b], rs_in.at[chip], rs_send, rs_recv,
                    device_id=device(x, b), device_id_type=MESH,
                ).start()

            return 0

        lax.fori_loop(q * per_part, (q + 1) * per_part, scatter, 0)

    rs_in[pl.ds(chip, 1)] = rbuf[pl.ds(chip, 1)]
    u[...] = jnp.zeros_like(u)
    gram[...] = jnp.zeros_like(gram)
    lengths, _, _, _ = bounds(len_ref, core)
    pltpu.make_async_remote_copy(
        rbuf.at[pl.ds(0, CHIPS - 1)], rs_in.at[pl.ds(0, CHIPS - 1)], rs_send, rs_recv,
        device_id=other_core, device_id_type=MESH,
    ).wait()
    total = jnp.sum(rs_in[...], axis=0)
    gain = w_ref[:, pl.ds(pl.multiple_of(chip * LANES, LANES), LANES)]
    pooled[chip, x, core] = total * gain / lengths

    def to_planes(dz, _):
        tile = pooled.at[chip, x, core]
        pltpu.make_async_remote_copy(
            tile, tile, z_send, z_recv.at[dz],
            device_id=device(x, lax.rem(z + dz, NZ) * NY + y), device_id_type=MESH,
        ).start()
        return 0

    def to_plane(dz):
        tile = pooled.at[lax.rem(z + NZ - dz, NZ) * NY + y, x, core]

        def step(i, _):
            pltpu.make_async_remote_copy(
                tile, tile, p_send, p_recv.at[dz], device_id=plane_peer(i), device_id_type=MESH
            ).start()
            return 0

        lax.fori_loop(1, PLANE, step, 0)

    lax.fori_loop(1, NZ, to_planes, 0)
    to_plane(0)
    for dz in NEAR_FIRST[1:]:
        tile = pooled.at[lax.rem(z + NZ - dz, NZ) * NY + y, x, core]
        pltpu.make_async_remote_copy(
            tile, tile, z_send, z_recv.at[dz], device_id=other_core, device_id_type=MESH
        ).wait_recv()
        to_plane(dz)

    def forward(dz):
        at = pl.ds(lax.rem(z + NZ - dz, NZ) * NY, NY)
        pltpu.make_async_remote_copy(
            rs_in.at[pl.ds(0, PLANE - 1)], rs_in.at[pl.ds(0, PLANE - 1)], p_send, p_recv.at[dz],
            device_id=other_core, device_id_type=MESH,
        ).wait_recv()
        copy = pltpu.make_async_remote_copy(
            pooled.at[at, :, core], pooled.at[at, :, core], f_send.at[dz], f_recv.at[dz],
            device_id=other_core, device_id_type=MESH,
        )
        copy.start()
        return copy

    def products(dz):
        plane = lax.rem(z + NZ - dz, NZ)
        columns = pl.ds(pl.multiple_of(plane * ZCOLS, ZCOLS), ZCOLS)
        value = jnp.concatenate(
            [pooled[plane * NY + i].reshape(NDOC, LANES) for i in range(NY)], axis=1
        )
        high, low = split(value)
        gram[...] += nt_dot(
            jnp.concatenate([high, high, low], axis=1), jnp.concatenate([high, low, high], axis=1)
        )
        high, low = split(value * w_ref[:, columns])
        both = jnp.concatenate([high, low], axis=0)
        ww_ref[:, columns] = both
        for o in range(2):
            u[o] += nt_dot(hv[o, :, columns], both)

    held = None
    for dz in NEAR_FIRST:
        copy = forward(dz)
        if held is not None:
            held[1].wait()
            products(held[0])
        held = (dz, copy)
    held[1].wait()
    products(held[0])

    k = lax.broadcasted_iota(jnp.int32, (NDOC, NDOC), 0)
    l = lax.broadcasted_iota(jnp.int32, (NDOC, NDOC), 1)
    eye = k == l
    table = gram[...]
    only = jnp.where(eye, table, 0.0)
    norm2 = jnp.sum(only, axis=1, keepdims=True) + EPS
    norms = jnp.sqrt(norm2) * jnp.sqrt(jnp.sum(only, axis=0, keepdims=True) + EPS)
    scaled = 1.0 / (norms * SHARPNESS)
    logits = table * scaled
    weights = jnp.where(eye, 0.0, jnp.exp(logits))
    sum_down = jnp.sum(weights, axis=1, keepdims=True)
    sum_along = jnp.sum(weights, axis=0, keepdims=True)
    pair = jnp.where(partner_ref[...] == k, 1.0, 0.0)
    target = jnp.sum(jnp.sum(pair * logits, axis=1, keepdims=True), axis=0, keepdims=True)
    logs = jnp.sum(jnp.log(sum_down), axis=0, keepdims=True)
    loss_ref[...] = (logs - target) * (1.0 / NDOC)
    change = (weights * (1.0 / sum_down + 1.0 / sum_along) - 2.0 * pair) * (1.0 / NDOC)
    own = jnp.sum(change * logits, axis=1, keepdims=True) / norm2
    sym[...] = change * scaled - jnp.where(eye, own, 0.0)

    place = (seq * TOK + lax.broadcasted_iota(jnp.int32, (TOK, 128), 0)).astype(F32)
    for o in range(2):
        lengths, _, _, start_along = bounds(len_ref, rows[o])
        ours = sym[pl.ds(pl.multiple_of((x * NCORE + rows[o]) * DOCS_ROW, DOCS_ROW), DOCS_ROW), :]
        ours = ours * (LOSS_SCALE / lengths)
        ours = jnp.concatenate([ours, ours], axis=1)
        mix = jnp.broadcast_to(ours[0:1], (TOK, 128))
        for d in range(1, DOCS_ROW):
            mix = jnp.where(place >= start_along[:, d : d + 1], ours[d : d + 1], mix)
        inner = jnp.sum(u[o] * mix, axis=1, keepdims=True) * (1.0 / D)
        inv = sb[o]
        a_ref[rows[o]] = inv * inv * inv * inner
        high, low = split(inv * mix)
        bb_ref[rows[o], :, 0:128] = high
        bb_ref[rows[o], :, 128:256] = low

    pltpu.make_async_copy(rs_in.at[pl.ds(0, NZ - 1)], rs_in.at[pl.ds(0, NZ - 1)], z_send).wait()
    for _ in range(NZ):
        pltpu.make_async_copy(
            rs_in.at[pl.ds(0, PLANE - 1)], rs_in.at[pl.ds(0, PLANE - 1)], p_send
        ).wait()


def grad_kernel(h_ref, bb_ref, a_ref, ww_ref, loss_ref, out_ref, loss_out):
    both = ww_ref[...]
    both = jnp.concatenate([both, both], axis=0)
    for r in range(2):
        for q in range(2):
            at = slice(q * 128, (q + 1) * 128)
            first = jnp.dot(bb_ref[r, at], both, preferred_element_type=F32)
            a = a_ref[r, at]
            a = jnp.concatenate([a] * (first.shape[1] // 128), axis=1)
            out_ref[r, at] = (first - h_ref[r, at].astype(F32) * a).astype(BF16)
    loss_out[...] = loss_ref[...]


def shards(hidden, doc_lengths, partner, closing_layer_weight):
    vmem = pl.BlockSpec(memory_space=pltpu.VMEM)
    dma = pltpu.SemaphoreType.DMA
    bb, a, ww, loss = pl.pallas_call(
        pool_kernel,
        out_shape=(
            jax.ShapeDtypeStruct((2, TOK, 256), BF16),
            jax.ShapeDtypeStruct((2, TOK, 128), F32),
            jax.ShapeDtypeStruct((2 * NDOC, D), BF16),
            jax.ShapeDtypeStruct((1, 1), F32),
        ),
        in_specs=[pl.BlockSpec(memory_space=pltpu.HBM), vmem, vmem, vmem],
        out_specs=(vmem, vmem, vmem, vmem),
        scratch_shapes=[
            pltpu.VMEM((2, TOK, D), BF16),
            pltpu.VMEM((2, TOK, 128), F32),
            pltpu.VMEM((CHIPS, DOCS_ROW, LANES), F32),
            pltpu.VMEM((CHIPS, DOCS_ROW, LANES), F32),
            pltpu.VMEM((CHIPS, DOCS_ROW, LANES), F32),
            pltpu.VMEM((CHIPS, DOCS_ROW, LANES), F32),
            pltpu.VMEM((CHIPS, NX, NCORE, DOCS_ROW, LANES), F32),
            pltpu.VMEM((2, TOK, 128), F32),
            pltpu.VMEM((NDOC, NDOC), F32),
            pltpu.VMEM((NDOC, NDOC), F32),
            dma((2 * PARTS,)),
            dma((PARTS,)), dma((PARTS,)),
            dma, dma,
            dma, dma((NZ,)),
            dma, dma((NZ,)),
            dma((NZ,)), dma((NZ,)),
        ],
        compiler_params=pltpu.CompilerParams(
            collective_id=0, has_side_effects=True, vmem_limit_bytes=20 * 1024 * 1024
        ),
        name="pool_and_loss",
    )(hidden, doc_lengths, partner.reshape(1, NDOC), closing_layer_weight.reshape(1, D))
    width = 512
    out, loss = pl.pallas_call(
        grad_kernel,
        grid=(D // width,),
        out_shape=(
            jax.ShapeDtypeStruct((2, TOK, D), BF16),
            jax.ShapeDtypeStruct((1, 1), F32),
        ),
        in_specs=[
            pl.BlockSpec((2, TOK, width), lambda i: (0, 0, i)),
            pl.BlockSpec((2, TOK, 256), lambda i: (0, 0, 0)),
            pl.BlockSpec((2, TOK, 128), lambda i: (0, 0, 0)),
            pl.BlockSpec((2 * NDOC, width), lambda i: (0, i)),
            pl.BlockSpec((1, 1), lambda i: (0, 0)),
        ],
        out_specs=(
            pl.BlockSpec((2, TOK, width), lambda i: (0, 0, i)),
            pl.BlockSpec((1, 1), lambda i: (0, 0)),
        ),
        compiler_params=pltpu.CompilerParams(vmem_limit_bytes=16 * 1024 * 1024),
        name="hidden_gradient",
    )(hidden, bb, a, ww, loss)
    return out, loss.reshape(())


def solution(mesh):
    in_specs = (P("dp", "seq", None), P("dp", None), P(), P())
    out_specs = (P("dp", "seq", None), P())
    return jax.shard_map(shards, mesh=mesh, in_specs=in_specs, out_specs=out_specs, check_vma=False)
```

```python
import jax
import jax.numpy as jnp
from jax import lax
from jax.experimental import pallas as pl
from jax.experimental.pallas import tpu as pltpu
from jax.sharding import PartitionSpec as P

MESH = pl.DeviceIdType.MESH
F32, BF16 = jnp.float32, jnp.bfloat16

SHARPNESS = 0.05
LOSS_SCALE = 524288.0
EPS = 1e-06

NX, NZ, NY, NCORE = 4, 8, 4, 2
CHIPS = NZ * NY
PLANE = NX * NY
D = 4096
DOCS_ROW = 8
NDOC = 64
TOK = 256
LANES = D // CHIPS
ZCOLS = LANES * NY
PARTS = 4
WIDTH = 512
NEAR_FIRST = (0, 1, 7, 2, 6, 3, 5, 4)


def bounds(len_ref, row):
    along = len_ref[pl.ds(row, 1), :].astype(F32)
    k = lax.broadcasted_iota(jnp.int32, (DOCS_ROW, DOCS_ROW), 0)
    l = lax.broadcasted_iota(jnp.int32, (DOCS_ROW, DOCS_ROW), 1)
    spread = jnp.broadcast_to(along, (DOCS_ROW, DOCS_ROW))
    down = jnp.sum(jnp.where(k == l, spread, 0.0), axis=1, keepdims=True)
    finish_down = jnp.sum(jnp.where(l <= k, spread, 0.0), axis=1, keepdims=True)
    start_down = finish_down - down
    start_along = jnp.sum(jnp.where(k < l, jnp.broadcast_to(down, (DOCS_ROW, DOCS_ROW)), 0.0), axis=0, keepdims=True)
    return down, start_down, finish_down, start_along


def split(value):
    high = value.astype(BF16)
    return high, (value - high.astype(F32)).astype(BF16)


def nt_dot(a, b):
    return lax.dot_general(a, b, (((1,), (1,)), ((), ())), preferred_element_type=F32)


def pool_kernel(
    h_hbm, len_hbm, partner_hbm, w_hbm,
    hv, bb_ref, a_ref, ww_ref, loss_ref,
    len_ref, partner_ref, w_ref, sb, csend, crecv, rbuf, rs_in, pooled, u, gram, sym,
    load_sem, small_sem, core_send, core_recv, rs_send, rs_recv, z_send, z_recv, p_send, p_recv, f_send, f_recv,
):
    x = lax.axis_index("dp")
    seq = lax.axis_index("seq")
    chip = lax.div(seq, NCORE)
    core = lax.rem(seq, NCORE)
    z = lax.div(chip, NY)
    y = lax.rem(chip, NY)
    rows = (1 - core, core)

    def device(to_x, to_chip):
        return (to_x, to_chip * NCORE + core)

    def plane_peer(i):
        q = lax.rem(x * NY + y + i, PLANE)
        return device(lax.div(q, NY), z * NY + lax.rem(q, NY))

    other_core = (x, chip * NCORE + 1 - core)

    loads = []
    for o in range(2):
        for q in range(PARTS):
            part = pl.ds(q * (TOK // PARTS), TOK // PARTS)
            copy = pltpu.make_async_copy(
                h_hbm.at[rows[o], part], hv.at[rows[o], part], load_sem.at[o * PARTS + q]
            )
            copy.start()
            loads.append(copy)
    small = []
    for n, (here, there) in enumerate(
        ((len_hbm, len_ref), (w_hbm, w_ref), (partner_hbm, partner_ref))
    ):
        copy = pltpu.make_async_copy(here, there, small_sem.at[n])
        copy.start()
        small.append(copy)

    barrier = pltpu.get_barrier_semaphore()

    def hello(i, _):
        to = device(x, lax.rem(chip + i, CHIPS))
        pl.semaphore_signal(barrier, inc=1, device_id=to, device_id_type=MESH)
        return 0

    def hello_plane(i, _):
        to = device(lax.rem(x + 1 + lax.div(i, NY), NX), z * NY + lax.rem(y + i, NY))
        pl.semaphore_signal(barrier, inc=1, device_id=to, device_id_type=MESH)
        return 0

    lax.fori_loop(1, CHIPS, hello, 0)
    lax.fori_loop(0, (NX - 1) * NY, hello_plane, 0)
    pl.semaphore_signal(barrier, inc=1, device_id=other_core, device_id_type=MESH)

    def squares(o, q):
        def step(n, _):
            at = pl.ds(pl.multiple_of(q * (TOK // PARTS) + n * 32, 32), 32)
            acc = jnp.zeros((32, 128), F32)
            for t in range(D // 128):
                v = hv[rows[o], at, t * 128 : (t + 1) * 128].astype(F32)
                acc = acc + v * v
            total = jnp.sum(acc, axis=1, keepdims=True)
            sb[o, at, :] = jnp.broadcast_to(lax.rsqrt(total * (1.0 / D) + EPS), (32, 128))
            return 0

        lax.fori_loop(0, TOK // PARTS // 32, step, 0)

    along = (seq * TOK + lax.broadcasted_iota(jnp.int32, (DOCS_ROW, TOK), 1)).astype(F32)

    def selector(o):
        _, start_down, finish_down, _ = bounds(len_ref, rows[o])
        inv = sb[o].T[0:DOCS_ROW, :]
        member = (along >= start_down) & (along < finish_down)
        high, low = split(jnp.where(member, inv, 0.0))
        return jnp.concatenate([high, low], axis=0)

    def sums(chosen, o, q):
        both = jnp.dot(
            chosen, hv[rows[o], :, q * (D // PARTS) : (q + 1) * (D // PARTS)], preferred_element_type=F32
        )
        return both[0:DOCS_ROW] + both[DOCS_ROW : 2 * DOCS_ROW]

    per_part = CHIPS // PARTS
    for q in range(PARTS):
        loads[q].wait()
        squares(0, q)
    for copy in small:
        copy.wait()
    chosen = selector(0)
    core_copies = []
    for q in range(PARTS):
        part = sums(chosen, 0, q)
        for b in range(per_part):
            csend[q * per_part + b] = part[:, b * LANES : (b + 1) * LANES]
        if q == 0:
            pl.semaphore_wait(barrier, CHIPS - 1 + (NX - 1) * NY + 1)
        at = pl.ds(q * per_part, per_part)
        copy = pltpu.make_async_remote_copy(
            csend.at[at], crecv.at[at], core_send.at[q], core_recv.at[q],
            device_id=other_core, device_id_type=MESH,
        )
        copy.start()
        core_copies.append(copy)
    for q in range(PARTS):
        loads[PARTS + q].wait()
        squares(1, q)
    chosen = selector(1)
    for q in range(PARTS):
        part = sums(chosen, 1, q)
        core_copies[q].wait()
        for b in range(per_part):
            rbuf[q * per_part + b] = part[:, b * LANES : (b + 1) * LANES] + crecv[q * per_part + b]

        def scatter(b, _):
            @pl.when(b != chip)
            def _():
                pltpu.make_async_remote_copy(
                    rbuf.at[b], rs_in.at[chip], rs_send, rs_recv,
                    device_id=device(x, b), device_id_type=MESH,
                ).start()

            return 0

        lax.fori_loop(q * per_part, (q + 1) * per_part, scatter, 0)

    rs_in[pl.ds(chip, 1)] = rbuf[pl.ds(chip, 1)]
    u[...] = jnp.zeros_like(u)
    gram[...] = jnp.zeros_like(gram)
    lengths, _, _, _ = bounds(len_ref, core)
    pltpu.make_async_remote_copy(
        rbuf.at[pl.ds(0, CHIPS - 1)], rs_in.at[pl.ds(0, CHIPS - 1)], rs_send, rs_recv,
        device_id=other_core, device_id_type=MESH,
    ).wait()
    total = jnp.sum(rs_in[...], axis=0)
    gain = w_ref[:, pl.ds(pl.multiple_of(chip * LANES, LANES), LANES)]
    pooled[chip, x, core] = total * gain / lengths

    def to_planes(dz, _):
        tile = pooled.at[chip, x, core]
        pltpu.make_async_remote_copy(
            tile, tile, z_send, z_recv.at[dz],
            device_id=device(x, lax.rem(z + dz, NZ) * NY + y), device_id_type=MESH,
        ).start()
        return 0

    def to_plane(dz):
        tile = pooled.at[lax.rem(z + NZ - dz, NZ) * NY + y, x, core]

        def step(i, _):
            pltpu.make_async_remote_copy(
                tile, tile, p_send, p_recv.at[dz], device_id=plane_peer(i), device_id_type=MESH
            ).start()
            return 0

        lax.fori_loop(1, PLANE, step, 0)

    lax.fori_loop(1, NZ, to_planes, 0)
    to_plane(0)
    for dz in NEAR_FIRST[1:]:
        tile = pooled.at[lax.rem(z + NZ - dz, NZ) * NY + y, x, core]
        pltpu.make_async_remote_copy(
            tile, tile, z_send, z_recv.at[dz], device_id=other_core, device_id_type=MESH
        ).wait_recv()
        to_plane(dz)

    def forward(dz):
        at = pl.ds(lax.rem(z + NZ - dz, NZ) * NY, NY)
        pltpu.make_async_remote_copy(
            rs_in.at[pl.ds(0, PLANE - 1)], rs_in.at[pl.ds(0, PLANE - 1)], p_send, p_recv.at[dz],
            device_id=other_core, device_id_type=MESH,
        ).wait_recv()
        copy = pltpu.make_async_remote_copy(
            pooled.at[at, :, core], pooled.at[at, :, core], f_send.at[dz], f_recv.at[dz],
            device_id=other_core, device_id_type=MESH,
        )
        copy.start()
        return copy

    def products(dz):
        plane = lax.rem(z + NZ - dz, NZ)
        columns = pl.ds(pl.multiple_of(plane * ZCOLS, ZCOLS), ZCOLS)
        value = jnp.concatenate(
            [pooled[plane * NY + i].reshape(NDOC, LANES) for i in range(NY)], axis=1
        )
        high, low = split(value)
        gram[...] += nt_dot(
            jnp.concatenate([high, high, low], axis=1), jnp.concatenate([high, low, high], axis=1)
        )
        high, low = split(value * w_ref[:, columns])
        both = jnp.concatenate([high, low], axis=0)
        ww_ref[:, columns] = both
        for o in range(2):
            u[o] += nt_dot(hv[rows[o], :, columns], both)

    held = None
    for dz in NEAR_FIRST:
        copy = forward(dz)
        if held is not None:
            held[1].wait()
            products(held[0])
        held = (dz, copy)
    held[1].wait()
    products(held[0])

    k = lax.broadcasted_iota(jnp.int32, (NDOC, NDOC), 0)
    l = lax.broadcasted_iota(jnp.int32, (NDOC, NDOC), 1)
    eye = k == l
    table = gram[...]
    only = jnp.where(eye, table, 0.0)
    norm2 = jnp.sum(only, axis=1, keepdims=True) + EPS
    norms = jnp.sqrt(norm2) * jnp.sqrt(jnp.sum(only, axis=0, keepdims=True) + EPS)
    scaled = 1.0 / (norms * SHARPNESS)
    logits = table * scaled
    weights = jnp.where(eye, 0.0, jnp.exp(logits))
    sum_down = jnp.sum(weights, axis=1, keepdims=True)
    sum_along = jnp.sum(weights, axis=0, keepdims=True)
    pair = jnp.where(partner_ref[...] == k, 1.0, 0.0)
    target = jnp.sum(jnp.sum(pair * logits, axis=1, keepdims=True), axis=0, keepdims=True)
    logs = jnp.sum(jnp.log(sum_down), axis=0, keepdims=True)
    loss_ref[...] = (logs - target) * (1.0 / NDOC)
    change = (weights * (1.0 / sum_down + 1.0 / sum_along) - 2.0 * pair) * (1.0 / NDOC)
    own = jnp.sum(change * logits, axis=1, keepdims=True) / norm2
    sym[...] = change * scaled - jnp.where(eye, own, 0.0)

    place = (seq * TOK + lax.broadcasted_iota(jnp.int32, (TOK, 128), 0)).astype(F32)
    for o in range(2):
        lengths, _, _, start_along = bounds(len_ref, rows[o])
        ours = sym[pl.ds(pl.multiple_of((x * NCORE + rows[o]) * DOCS_ROW, DOCS_ROW), DOCS_ROW), :]
        ours = ours * (LOSS_SCALE / lengths)
        ours = jnp.concatenate([ours, ours], axis=1)
        mix = jnp.broadcast_to(ours[0:1], (TOK, 128))
        for d in range(1, DOCS_ROW):
            mix = jnp.where(place >= start_along[:, d : d + 1], ours[d : d + 1], mix)
        inner = jnp.sum(u[o] * mix, axis=1, keepdims=True) * (1.0 / D)
        inv = sb[o]
        a_ref[rows[o]] = inv * inv * inv * inner
        high, low = split(inv * mix)
        bb_ref[rows[o], :, 0:128] = high
        bb_ref[rows[o], :, 128:256] = low

    pltpu.make_async_copy(rs_in.at[pl.ds(0, NZ - 1)], rs_in.at[pl.ds(0, NZ - 1)], z_send).wait()
    for _ in range(NZ):
        pltpu.make_async_copy(
            rs_in.at[pl.ds(0, PLANE - 1)], rs_in.at[pl.ds(0, PLANE - 1)], p_send
        ).wait()


def grad_kernel(h_ref, bb_ref, a_ref, ww_ref, loss_ref, out_hbm, loss_out, out, sem):
    copies = []
    for n in range(D // WIDTH):
        columns = slice(n * WIDTH, (n + 1) * WIDTH)
        both = ww_ref[:, columns]
        both = jnp.concatenate([both, both], axis=0)
        for r in range(2):
            first = jnp.dot(bb_ref[r], both, preferred_element_type=F32)
            a = jnp.concatenate([a_ref[r]] * (WIDTH // 128), axis=1)
            out[r, :, columns] = (first - h_ref[r, :, columns].astype(F32) * a).astype(BF16)
        copy = pltpu.make_async_copy(out.at[:, :, columns], out_hbm.at[:, :, columns], sem.at[n])
        copy.start()
        copies.append(copy)
    loss_out[...] = loss_ref[...]
    for copy in copies:
        copy.wait()


def shards(hidden, doc_lengths, partner, closing_layer_weight):
    vmem = pl.BlockSpec(memory_space=pltpu.VMEM)
    hbm = pl.BlockSpec(memory_space=pltpu.HBM)
    dma = pltpu.SemaphoreType.DMA
    arguments = (hidden, doc_lengths, partner.reshape(1, NDOC), closing_layer_weight.reshape(1, D))
    h, bb, a, ww, loss = pl.pallas_call(
        pool_kernel,
        out_shape=(
            pltpu.VMEM((2, TOK, D), BF16),
            pltpu.VMEM((2, TOK, 256), BF16),
            pltpu.VMEM((2, TOK, 128), F32),
            pltpu.VMEM((2 * NDOC, D), BF16),
            jax.ShapeDtypeStruct((1, 1), F32),
        ),
        in_specs=[hbm] * 4,
        out_specs=(vmem,) * 5,
        scratch_shapes=[
            pltpu.VMEM((2, DOCS_ROW), jnp.int32),
            pltpu.VMEM((1, NDOC), jnp.int32),
            pltpu.VMEM((1, D), F32),
            pltpu.VMEM((2, TOK, 128), F32),
            pltpu.VMEM((CHIPS, DOCS_ROW, LANES), F32),
            pltpu.VMEM((CHIPS, DOCS_ROW, LANES), F32),
            pltpu.VMEM((CHIPS, DOCS_ROW, LANES), F32),
            pltpu.VMEM((CHIPS, DOCS_ROW, LANES), F32),
            pltpu.VMEM((CHIPS, NX, NCORE, DOCS_ROW, LANES), F32),
            pltpu.VMEM((2, TOK, 128), F32),
            pltpu.VMEM((NDOC, NDOC), F32),
            pltpu.VMEM((NDOC, NDOC), F32),
            dma((2 * PARTS,)), dma((3,)),
            dma((PARTS,)), dma((PARTS,)),
            dma, dma,
            dma, dma((NZ,)),
            dma, dma((NZ,)),
            dma((NZ,)), dma((NZ,)),
        ],
        compiler_params=pltpu.CompilerParams(
            collective_id=0, has_side_effects=True, vmem_limit_bytes=16 * 1024 * 1024
        ),
        name="pool_and_loss",
    )(*(pltpu.with_memory_space_constraint(v, pltpu.HBM) for v in arguments))
    out, loss = pl.pallas_call(
        grad_kernel,
        out_shape=(
            jax.ShapeDtypeStruct((2, TOK, D), BF16),
            jax.ShapeDtypeStruct((1, 1), F32),
        ),
        in_specs=[vmem] * 5,
        out_specs=(pl.BlockSpec(memory_space=pl.ANY), vmem),
        scratch_shapes=[pltpu.VMEM((2, TOK, D), BF16), dma((D // WIDTH,))],
        compiler_params=pltpu.CompilerParams(vmem_limit_bytes=16 * 1024 * 1024),
        name="hidden_gradient",
    )(h, bb, a, ww, loss)
    return out, loss.reshape(())


def solution(mesh):
    in_specs = (P("dp", "seq", None), P("dp", None), P(), P())
    out_specs = (P("dp", "seq", None), P())
    return jax.shard_map(shards, mesh=mesh, in_specs=in_specs, out_specs=out_specs, check_vma=False)
```

```python
import jax
import jax.numpy as jnp
from jax import lax
from jax.experimental import pallas as pl
from jax.experimental.pallas import tpu as pltpu
from jax.sharding import PartitionSpec as P

MESH = pl.DeviceIdType.MESH
F32, BF16 = jnp.float32, jnp.bfloat16

SHARPNESS = 0.05
LOSS_SCALE = 524288.0
EPS = 1e-06

NX, NZ, NY, NCORE = 4, 8, 4, 2
CHIPS = NZ * NY
PLANE = NX * NY
D = 4096
DOCS_ROW = 8
NDOC = 64
TOK = 256
LANES = D // CHIPS
ZCOLS = LANES * NY
PARTS = 4
WIDTH = 512
NEAR_FIRST = (0, 1, 7, 2, 6, 3, 5, 4)
BOTH = (3, 5, 4)
IN_FLIGHT = 8


def offsets(dz):
    found = []
    for i in range(1, PLANE * NCORE):
        dx, dy, dc = i // (NY * NCORE), i // NCORE % NY, i % NCORE
        if dz in BOTH or dc == 0:
            found.append((dx, dy, dc))
    return sorted(found, key=lambda t: -min(t[0], NX - t[0]) - min(t[1], NY - t[1]))


def bounds(len_ref, row):
    along = len_ref[pl.ds(row, 1), :].astype(F32)
    k = lax.broadcasted_iota(jnp.int32, (DOCS_ROW, DOCS_ROW), 0)
    l = lax.broadcasted_iota(jnp.int32, (DOCS_ROW, DOCS_ROW), 1)
    spread = jnp.broadcast_to(along, (DOCS_ROW, DOCS_ROW))
    down = jnp.sum(jnp.where(k == l, spread, 0.0), axis=1, keepdims=True)
    finish_down = jnp.sum(jnp.where(l <= k, spread, 0.0), axis=1, keepdims=True)
    start_down = finish_down - down
    start_along = jnp.sum(jnp.where(k < l, jnp.broadcast_to(down, (DOCS_ROW, DOCS_ROW)), 0.0), axis=0, keepdims=True)
    return down, start_down, finish_down, start_along


def split(value):
    high = value.astype(BF16)
    return high, (value - high.astype(F32)).astype(BF16)


def nt_dot(a, b):
    return lax.dot_general(a, b, (((1,), (1,)), ((), ())), preferred_element_type=F32)


def pool_kernel(
    h_hbm, len_hbm, partner_hbm, w_hbm,
    hv, bb_ref, a_ref, ww_ref, loss_ref,
    len_ref, partner_ref, w_ref, sb, csend, crecv, rbuf, rs_in, pooled, u, gram, sym,
    load_sem, small_sem, core_send, core_recv, rs_send, rs_recv, z_send, z_recv, p_send, p_recv, f_send, f_recv,
):
    x = lax.axis_index("dp")
    seq = lax.axis_index("seq")
    chip = lax.div(seq, NCORE)
    core = lax.rem(seq, NCORE)
    z = lax.div(chip, NY)
    y = lax.rem(chip, NY)
    rows = (1 - core, core)

    def device(to_x, to_chip, to_core=core):
        return (to_x, to_chip * NCORE + to_core)

    def offset(dx, dz, dy, dc=None):
        return device(
            lax.rem(x + dx, NX),
            lax.rem(z + dz, NZ) * NY + lax.rem(y + dy, NY),
            lax.rem(core + dc, NCORE) if dc is not None else core,
        )

    def in_plane(i):
        return offset(lax.div(i, NY * NCORE), 0, lax.rem(lax.div(i, NCORE), NY), lax.rem(i, NCORE))

    other_core = (x, chip * NCORE + 1 - core)

    loads = []
    for o in range(2):
        for q in range(PARTS):
            part = pl.ds(q * (TOK // PARTS), TOK // PARTS)
            copy = pltpu.make_async_copy(
                h_hbm.at[rows[o], part], hv.at[rows[o], part], load_sem.at[o * PARTS + q]
            )
            loads.append(copy)
    for copy in loads[:IN_FLIGHT]:
        copy.start()
    small = []
    for n, (here, there) in enumerate(
        ((len_hbm, len_ref), (w_hbm, w_ref), (partner_hbm, partner_ref))
    ):
        copy = pltpu.make_async_copy(here, there, small_sem.at[n])
        copy.start()
        small.append(copy)

    barrier = pltpu.get_barrier_semaphore()

    def greet(to):
        pl.semaphore_signal(barrier, inc=1, device_id=to, device_id_type=MESH)

    def hello_plane(i, _):
        greet(in_plane(i))
        return 0

    def hello_column(i, _):
        greet(offset(0, lax.div(i, NY), lax.rem(i, NY)))
        return 0

    lax.fori_loop(NY, CHIPS, hello_column, 0)
    lax.fori_loop(1, PLANE * NCORE, hello_plane, 0)

    def squares(o, q):
        n = o * PARTS + q
        loads[n].wait()
        if n + IN_FLIGHT < len(loads):
            loads[n + IN_FLIGHT].start()
        at = pl.ds(q * (TOK // PARTS), TOK // PARTS)
        acc = jnp.zeros((TOK // PARTS, 128), F32)
        for t in range(D // 128):
            v = hv[rows[o], at, t * 128 : (t + 1) * 128].astype(F32)
            acc = acc + v * v
        sb[o, at, :] = acc

    along = (seq * TOK + lax.broadcasted_iota(jnp.int32, (DOCS_ROW, TOK), 1)).astype(F32)

    def selector(o):
        _, start_down, finish_down, _ = bounds(len_ref, rows[o])
        inv = lax.rsqrt(jnp.sum(sb[o].T, axis=0, keepdims=True) * (1.0 / D) + EPS)
        member = (along >= start_down) & (along < finish_down)
        high, low = split(jnp.where(member, inv, 0.0))
        return jnp.concatenate([high, low], axis=0)

    def sums(chosen, o, part):
        columns = pl.ds(pl.multiple_of(part * (D // PARTS), D // PARTS), D // PARTS)
        both = jnp.dot(chosen, hv[rows[o], :, columns], preferred_element_type=F32)
        return both[0:DOCS_ROW] + both[DOCS_ROW : 2 * DOCS_ROW]

    per_part = CHIPS // PARTS
    order = [lax.rem(lax.div(z * PARTS, NZ) + n, PARTS) for n in (2, 1, 3, 0)]
    for q in range(PARTS):
        squares(0, q)
    for copy in small:
        copy.wait()
    chosen = selector(0)
    core_copies = []
    for q, part in enumerate(order):
        value = sums(chosen, 0, part)
        for b in range(per_part):
            csend[part * per_part + b] = value[:, b * LANES : (b + 1) * LANES]
        if q == 0:
            pl.semaphore_wait(barrier, CHIPS - NY + PLANE * NCORE - 1)
        at = pl.ds(part * per_part, per_part)
        copy = pltpu.make_async_remote_copy(
            csend.at[at], crecv.at[at], core_send.at[q], core_recv.at[q],
            device_id=other_core, device_id_type=MESH,
        )
        copy.start()
        core_copies.append(copy)
    for q in range(PARTS):
        squares(1, q)
    chosen = selector(1)
    for q, part in enumerate(order):
        value = sums(chosen, 1, part)
        core_copies[q].wait()
        for b in range(per_part):
            to = part * per_part + b
            rbuf[to] = value[:, b * LANES : (b + 1) * LANES] + crecv[to]

            def scatter(to=to):
                pltpu.make_async_remote_copy(
                    rbuf.at[to], rs_in.at[chip], rs_send, rs_recv,
                    device_id=device(x, to), device_id_type=MESH,
                ).start()

            if q + 1 < PARTS:
                scatter()
            else:
                pl.when(to != chip)(scatter)

    rs_in[pl.ds(chip, 1)] = rbuf[pl.ds(chip, 1)]
    for o in range(2):
        square = jnp.sum(sb[o], axis=1, keepdims=True) * (1.0 / D)
        sb[o] = jnp.broadcast_to(lax.rsqrt(square + EPS), (TOK, 128))
    u[...] = jnp.zeros_like(u)
    gram[...] = jnp.zeros_like(gram)
    lengths, _, _, _ = bounds(len_ref, core)
    pltpu.make_async_remote_copy(
        rbuf.at[pl.ds(0, CHIPS - 1)], rs_in.at[pl.ds(0, CHIPS - 1)], rs_send, rs_recv,
        device_id=other_core, device_id_type=MESH,
    ).wait()
    total = jnp.sum(rs_in[...], axis=0)
    gain = w_ref[:, pl.ds(pl.multiple_of(chip * LANES, LANES), LANES)]
    pooled[chip, x, core] = total * gain / lengths

    mine = pooled.at[chip, x, core]

    def passed(dz):
        return pooled.at[lax.rem(z + NZ - dz, NZ) * NY + y, x, core]

    def send(tile, dz, to):
        pltpu.make_async_remote_copy(
            tile, tile, p_send, p_recv.at[dz], device_id=to, device_id_type=MESH
        ).start()

    def to_plane(dz):
        tile = passed(dz)
        for dx, dy, dc in offsets(dz):
            send(tile, dz, offset(dx, 0, dy, dc))

    for dz in NEAR_FIRST[:0:-1]:
        pltpu.make_async_remote_copy(
            mine, mine, z_send, z_recv.at[dz], device_id=offset(0, dz, 0), device_id_type=MESH
        ).start()
    to_plane(0)
    for dz in NEAR_FIRST[1:]:
        tile = passed(dz)
        pltpu.make_async_remote_copy(
            tile, tile, z_send, z_recv.at[dz], device_id=other_core, device_id_type=MESH
        ).wait_recv()
        to_plane(dz)

    def take(dz):
        got = pl.ds(0, PLANE * NCORE - 1 if dz in BOTH else PLANE - 1)
        pltpu.make_async_remote_copy(
            rs_in.at[got], rs_in.at[got], p_send, p_recv.at[dz],
            device_id=other_core, device_id_type=MESH,
        ).wait_recv()
        if dz in BOTH:
            return None
        at = pl.ds(lax.rem(z + NZ - dz, NZ) * NY, NY)
        copy = pltpu.make_async_remote_copy(
            pooled.at[at, :, core], pooled.at[at, :, core], f_send.at[dz], f_recv.at[dz],
            device_id=other_core, device_id_type=MESH,
        )
        copy.start()
        return copy

    def products(dz):
        plane = lax.rem(z + NZ - dz, NZ)
        columns = pl.ds(pl.multiple_of(plane * ZCOLS, ZCOLS), ZCOLS)
        value = jnp.concatenate(
            [pooled[plane * NY + i].reshape(NDOC, LANES) for i in range(NY)], axis=1
        )
        high, low = split(value)
        gram[...] += nt_dot(
            jnp.concatenate([high, high, low], axis=1), jnp.concatenate([high, low, high], axis=1)
        )
        high, low = split(value * w_ref[:, columns])
        both = jnp.concatenate([high, low], axis=0)
        ww_ref[:, columns] = both
        for o in range(2):
            u[o] += nt_dot(hv[rows[o], :, columns], both)

    held = []
    for dz in NEAR_FIRST:
        copy = take(dz)
        if copy is not None:
            held.append((dz, copy))
            if len(held) < 2:
                continue
        while len(held) > (copy is not None):
            first, given = held.pop(0)
            given.wait()
            products(first)
        if copy is None:
            products(dz)
    for first, given in held:
        given.wait()
        products(first)

    k = lax.broadcasted_iota(jnp.int32, (NDOC, NDOC), 0)
    l = lax.broadcasted_iota(jnp.int32, (NDOC, NDOC), 1)
    eye = k == l
    table = gram[...]
    only = jnp.where(eye, table, 0.0)
    norm2 = jnp.sum(only, axis=1, keepdims=True) + EPS
    norms = jnp.sqrt(norm2) * jnp.sqrt(jnp.sum(only, axis=0, keepdims=True) + EPS)
    scaled = 1.0 / (norms * SHARPNESS)
    logits = table * scaled
    weights = jnp.where(eye, 0.0, jnp.exp(logits))
    sum_down = jnp.sum(weights, axis=1, keepdims=True)
    sum_along = jnp.sum(weights, axis=0, keepdims=True)
    pair = jnp.where(partner_ref[...] == k, 1.0, 0.0)
    target = jnp.sum(jnp.sum(pair * logits, axis=1, keepdims=True), axis=0, keepdims=True)
    logs = jnp.sum(jnp.log(sum_down), axis=0, keepdims=True)
    loss_ref[...] = (logs - target) * (1.0 / NDOC)
    change = (weights * (1.0 / sum_down + 1.0 / sum_along) - 2.0 * pair) * (1.0 / NDOC)
    own = jnp.sum(change * logits, axis=1, keepdims=True) / norm2
    sym[...] = change * scaled - jnp.where(eye, own, 0.0)

    place = (seq * TOK + lax.broadcasted_iota(jnp.int32, (TOK, 128), 0)).astype(F32)
    for o in range(2):
        lengths, _, _, start_along = bounds(len_ref, rows[o])
        ours = sym[pl.ds(pl.multiple_of((x * NCORE + rows[o]) * DOCS_ROW, DOCS_ROW), DOCS_ROW), :]
        ours = ours * (LOSS_SCALE / lengths)
        ours = jnp.concatenate([ours, ours], axis=1)
        mix = jnp.broadcast_to(ours[0:1], (TOK, 128))
        for d in range(1, DOCS_ROW):
            mix = jnp.where(place >= start_along[:, d : d + 1], ours[d : d + 1], mix)
        inner = jnp.sum(u[o] * mix, axis=1, keepdims=True) * (1.0 / D)
        inv = sb[o]
        a_ref[rows[o]] = inv * inv * inv * inner
        high, low = split(inv * mix)
        bb_ref[rows[o], :, 0:128] = high
        bb_ref[rows[o], :, 128:256] = low

    pltpu.make_async_copy(rs_in.at[pl.ds(0, NZ - 1)], rs_in.at[pl.ds(0, NZ - 1)], z_send).wait()
    left = sum(len(offsets(dz)) for dz in NEAR_FIRST)
    while left:
        some = pl.ds(0, min(left, CHIPS))
        pltpu.make_async_copy(rs_in.at[some], rs_in.at[some], p_send).wait()
        left -= min(left, CHIPS)


def grad_kernel(h_ref, bb_ref, a_ref, ww_ref, loss_ref, out_hbm, loss_out, out, sem):
    copies = [pltpu.make_async_copy(loss_ref, loss_out, sem.at[D // WIDTH])]
    copies[0].start()
    for n in range(D // WIDTH):
        columns = slice(n * WIDTH, (n + 1) * WIDTH)
        both = ww_ref[:, columns]
        both = jnp.concatenate([both, both], axis=0)
        for r in range(2):
            first = jnp.dot(bb_ref[r], both, preferred_element_type=F32)
            a = jnp.concatenate([a_ref[r]] * (WIDTH // 128), axis=1)
            out[r, :, columns] = (first - h_ref[r, :, columns].astype(F32) * a).astype(BF16)
        copy = pltpu.make_async_copy(out.at[:, :, columns], out_hbm.at[:, :, columns], sem.at[n])
        copy.start()
        copies.append(copy)
    for copy in copies:
        copy.wait()


def shards(hidden, doc_lengths, partner, closing_layer_weight):
    vmem = pl.BlockSpec(memory_space=pltpu.VMEM)
    hbm = pl.BlockSpec(memory_space=pltpu.HBM)
    dma = pltpu.SemaphoreType.DMA
    arguments = (hidden, doc_lengths, partner.reshape(1, NDOC), closing_layer_weight.reshape(1, D))
    h, bb, a, ww, loss = pl.pallas_call(
        pool_kernel,
        out_shape=(
            pltpu.VMEM((2, TOK, D), BF16),
            pltpu.VMEM((2, TOK, 256), BF16),
            pltpu.VMEM((2, TOK, 128), F32),
            pltpu.VMEM((2 * NDOC, D), BF16),
            pltpu.VMEM((1, 1), F32),
        ),
        in_specs=[hbm] * 4,
        out_specs=(vmem,) * 5,
        scratch_shapes=[
            pltpu.VMEM((2, DOCS_ROW), jnp.int32),
            pltpu.VMEM((1, NDOC), jnp.int32),
            pltpu.VMEM((1, D), F32),
            pltpu.VMEM((2, TOK, 128), F32),
            pltpu.VMEM((CHIPS, DOCS_ROW, LANES), F32),
            pltpu.VMEM((CHIPS, DOCS_ROW, LANES), F32),
            pltpu.VMEM((CHIPS, DOCS_ROW, LANES), F32),
            pltpu.VMEM((CHIPS, DOCS_ROW, LANES), F32),
            pltpu.VMEM((CHIPS, NX, NCORE, DOCS_ROW, LANES), F32),
            pltpu.VMEM((2, TOK, 128), F32),
            pltpu.VMEM((NDOC, NDOC), F32),
            pltpu.VMEM((NDOC, NDOC), F32),
            dma((2 * PARTS,)), dma((3,)),
            dma((PARTS,)), dma((PARTS,)),
            dma, dma,
            dma, dma((NZ,)),
            dma, dma((NZ,)),
            dma((NZ,)), dma((NZ,)),
        ],
        compiler_params=pltpu.CompilerParams(
            collective_id=0, has_side_effects=True, vmem_limit_bytes=16 * 1024 * 1024
        ),
        name="pool_and_loss",
    )(*(pltpu.with_memory_space_constraint(v, pltpu.HBM) for v in arguments))
    out, loss = pl.pallas_call(
        grad_kernel,
        out_shape=(
            jax.ShapeDtypeStruct((2, TOK, D), BF16),
            jax.ShapeDtypeStruct((1, 1), F32),
        ),
        in_specs=[vmem] * 5,
        out_specs=(pl.BlockSpec(memory_space=pl.ANY),) * 2,
        scratch_shapes=[pltpu.VMEM((2, TOK, D), BF16), dma((D // WIDTH + 1,))],
        compiler_params=pltpu.CompilerParams(vmem_limit_bytes=16 * 1024 * 1024),
        name="hidden_gradient",
    )(h, bb, a, ww, loss)
    return out, loss.reshape(())


def solution(mesh):
    in_specs = (P("dp", "seq", None), P("dp", None), P(), P())
    out_specs = (P("dp", "seq", None), P())
    return jax.shard_map(shards, mesh=mesh, in_specs=in_specs, out_specs=out_specs, check_vma=False)
```

```python
import jax
import jax.numpy as jnp
from jax import lax
from jax.experimental import pallas as pl
from jax.experimental.pallas import tpu as pltpu
from jax.sharding import PartitionSpec as P

MESH = pl.DeviceIdType.MESH
F32, BF16 = jnp.float32, jnp.bfloat16

SHARPNESS = 0.05
LOSS_SCALE = 524288.0
EPS = 1e-06

NX, NZ, NY, NCORE = 4, 8, 4, 2
CHIPS = NZ * NY
PLANE = NX * NY
D = 4096
DOCS_ROW = 8
NDOC = 64
TOK = 256
LANES = D // CHIPS
ZCOLS = LANES * NY
PARTS = 4
WIDTH = 512
BOTH = (4, 3)
WHOLE = (1, 7)
RELAYED = (2, 6, 3, 5, 4)
TAKEN = (0, 2, 6, 1, 7, 3, 5, 4)
IN_FLIGHT = 8


def offsets(dz):
    found = []
    for i in range(1, PLANE * NCORE):
        dx, dy, dc = i // (NY * NCORE), i // NCORE % NY, i % NCORE
        if dz in BOTH or dc == 0:
            found.append((dx, dy, dc))
    return sorted(found, key=lambda t: -min(t[0], NX - t[0]) - min(t[1], NY - t[1]))


def peers():
    found = [(dz, 0, dy, 0) for dz in range(1, NZ) for dy in range(NY)]
    found += [(0, *at) for at in offsets(BOTH[0])] + [(dz, 0, 0, 1) for dz in WHOLE]

    def hops(t):
        return min(t[0], NZ - t[0]) + min(t[1], NX - t[1]) + min(t[2], NY - t[2])

    return sorted(found, key=lambda t: -hops(t))


PEERS = peers()
NEXT = 16


def bounds(len_ref, row):
    along = len_ref[pl.ds(row, 1), :].astype(F32)
    k = lax.broadcasted_iota(jnp.int32, (DOCS_ROW, DOCS_ROW), 0)
    l = lax.broadcasted_iota(jnp.int32, (DOCS_ROW, DOCS_ROW), 1)
    spread = jnp.broadcast_to(along, (DOCS_ROW, DOCS_ROW))
    down = jnp.sum(jnp.where(k == l, spread, 0.0), axis=1, keepdims=True)
    finish_down = jnp.sum(jnp.where(l <= k, spread, 0.0), axis=1, keepdims=True)
    start_down = finish_down - down
    start_along = jnp.sum(jnp.where(k < l, jnp.broadcast_to(down, (DOCS_ROW, DOCS_ROW)), 0.0), axis=0, keepdims=True)
    return down, start_down, finish_down, start_along


def split(value):
    high = value.astype(BF16)
    return high, (value - high.astype(F32)).astype(BF16)


def nt_dot(a, b):
    return lax.dot_general(a, b, (((1,), (1,)), ((), ())), preferred_element_type=F32)


def pool_kernel(
    h_hbm, len_hbm, partner_hbm, w_hbm,
    hv, bb_ref, a_ref, ww_ref, loss_ref,
    len_ref, partner_ref, w_ref, sb, csend, crecv, rbuf, rs_in, pooled, u, gram, sym,
    load_sem, small_sem, core_send, core_recv, rs_send, rs_recv, z_send, z_recv, p_send, p_recv, f_send, f_recv, n_send,
):
    x = lax.axis_index("dp")
    seq = lax.axis_index("seq")
    chip = lax.div(seq, NCORE)
    core = lax.rem(seq, NCORE)
    z = lax.div(chip, NY)
    y = lax.rem(chip, NY)
    rows = (1 - core, core)

    def device(to_x, to_chip, to_core=core):
        return (to_x, to_chip * NCORE + to_core)

    def offset(dx, dz, dy, dc=None):
        return device(
            lax.rem(x + dx, NX),
            lax.rem(z + dz, NZ) * NY + lax.rem(y + dy, NY),
            lax.rem(core + dc, NCORE) if dc is not None else core,
        )

    other_core = (x, chip * NCORE + 1 - core)

    barrier = pltpu.get_barrier_semaphore()

    def greet(to):
        pl.semaphore_signal(barrier, inc=1, device_id=to, device_id_type=MESH)

    for dz, dx, dy, dc in PEERS[:NEXT]:
        greet(offset(dx, dz, dy, dc))

    small = []
    for n, (here, there) in enumerate(
        ((len_hbm, len_ref), (w_hbm, w_ref), (partner_hbm, partner_ref))
    ):
        copy = pltpu.make_async_copy(here, there, small_sem.at[n])
        copy.start()
        small.append(copy)
    loads = []
    for o in range(2):
        for q in range(PARTS):
            part = pl.ds(q * (TOK // PARTS), TOK // PARTS)
            copy = pltpu.make_async_copy(
                h_hbm.at[rows[o], part], hv.at[rows[o], part], load_sem.at[o * PARTS + q]
            )
            loads.append(copy)
    for copy in loads[:IN_FLIGHT]:
        copy.start()

    for dz, dx, dy, dc in PEERS[NEXT:]:
        greet(offset(dx, dz, dy, dc))

    def squares(o, q):
        n = o * PARTS + q
        loads[n].wait()
        if n + IN_FLIGHT < len(loads):
            loads[n + IN_FLIGHT].start()
        at = pl.ds(q * (TOK // PARTS), TOK // PARTS)
        acc = jnp.zeros((TOK // PARTS, 128), F32)
        for t in range(D // 128):
            v = hv[rows[o], at, t * 128 : (t + 1) * 128].astype(F32)
            acc = acc + v * v
        sb[o, at, :] = acc

    along = (seq * TOK + lax.broadcasted_iota(jnp.int32, (DOCS_ROW, TOK), 1)).astype(F32)

    def selector(o):
        _, start_down, finish_down, _ = bounds(len_ref, rows[o])
        inv = lax.rsqrt(jnp.sum(sb[o].T, axis=0, keepdims=True) * (1.0 / D) + EPS)
        member = (along >= start_down) & (along < finish_down)
        high, low = split(jnp.where(member, inv, 0.0))
        return jnp.concatenate([high, low], axis=0)

    def sums(chosen, o, part):
        columns = pl.ds(pl.multiple_of(part * (D // PARTS), D // PARTS), D // PARTS)
        both = jnp.dot(chosen, hv[rows[o], :, columns], preferred_element_type=F32)
        return both[0:DOCS_ROW] + both[DOCS_ROW : 2 * DOCS_ROW]

    per_part = CHIPS // PARTS
    order = [lax.rem(lax.div(z * PARTS, NZ) + n, PARTS) for n in (2, 1, 3, 0)]
    for q in range(PARTS):
        squares(0, q)
    for copy in small:
        copy.wait()
    chosen = selector(0)
    for part in order:
        value = sums(chosen, 0, part)
        for b in range(per_part):
            csend[part * per_part + b] = value[:, b * LANES : (b + 1) * LANES]
    for q in range(PARTS):
        squares(1, q)
    chosen = selector(1)
    for part in order:
        value = sums(chosen, 1, part)
        for b in range(per_part):
            rbuf[part * per_part + b] = value[:, b * LANES : (b + 1) * LANES]
    pl.semaphore_wait(barrier, len(PEERS))
    core_copies = []
    for q, part in enumerate(order):
        at = pl.ds(part * per_part, per_part)
        copy = pltpu.make_async_remote_copy(
            csend.at[at], crecv.at[at], core_send.at[q], core_recv.at[q],
            device_id=other_core, device_id_type=MESH,
        )
        copy.start()
        core_copies.append(copy)
    for q, part in enumerate(order):
        core_copies[q].wait_recv()
        at = pl.ds(part * per_part, per_part)
        rbuf[at] = rbuf[at] + crecv[at]
        for b in range(per_part):
            to = part * per_part + b

            def scatter(to=to):
                pltpu.make_async_remote_copy(
                    rbuf.at[to], rs_in.at[chip], rs_send, rs_recv,
                    device_id=device(x, to), device_id_type=MESH,
                ).start()

            if q + 1 < PARTS:
                scatter()
            else:
                pl.when(to != chip)(scatter)
    for copy in core_copies:
        copy.wait_send()

    rs_in[pl.ds(chip, 1)] = rbuf[pl.ds(chip, 1)]
    for o in range(2):
        square = jnp.sum(sb[o], axis=1, keepdims=True) * (1.0 / D)
        sb[o] = jnp.broadcast_to(lax.rsqrt(square + EPS), (TOK, 128))
    u[...] = jnp.zeros_like(u)
    gram[...] = jnp.zeros_like(gram)
    lengths, _, _, _ = bounds(len_ref, core)
    pltpu.make_async_remote_copy(
        rbuf.at[pl.ds(0, CHIPS - 1)], rs_in.at[pl.ds(0, CHIPS - 1)], rs_send, rs_recv,
        device_id=other_core, device_id_type=MESH,
    ).wait()
    total = jnp.sum(rs_in[...], axis=0)
    gain = w_ref[:, pl.ds(pl.multiple_of(chip * LANES, LANES), LANES)]
    pooled[chip, x, core] = total * gain / lengths

    mine = pooled.at[chip, x, core]

    def passed(dz):
        return pooled.at[lax.rem(z + NZ - dz, NZ) * NY + y, x, core]

    def send(tile, dz, to):
        pltpu.make_async_remote_copy(
            tile, tile, p_send, p_recv.at[dz], device_id=to, device_id_type=MESH
        ).start()

    def to_plane(dz):
        tile = passed(dz)
        for dx, dy, dc in offsets(dz):
            send(tile, dz, offset(dx, 0, dy, dc))

    for dz in RELAYED[::-1]:
        pltpu.make_async_remote_copy(
            mine, mine, z_send, z_recv.at[dz], device_id=offset(0, dz, 0), device_id_type=MESH
        ).start()
    to_plane(0)
    for dz in RELAYED:
        tile = passed(dz)
        pltpu.make_async_remote_copy(
            tile, tile, z_send, z_recv.at[dz], device_id=other_core, device_id_type=MESH
        ).wait_recv()
        to_plane(dz)

    def take(dz):
        parts = PLANE * NCORE if dz in WHOLE else PLANE * NCORE - 1 if dz in BOTH else PLANE - 1
        got = pl.ds(0, parts)
        pltpu.make_async_remote_copy(
            rs_in.at[got], rs_in.at[got], p_send, p_recv.at[dz],
            device_id=other_core, device_id_type=MESH,
        ).wait_recv()
        if dz in BOTH or dz in WHOLE:
            return None
        at = pl.ds(lax.rem(z + NZ - dz, NZ) * NY, NY)
        copy = pltpu.make_async_remote_copy(
            pooled.at[at, :, core], pooled.at[at, :, core], f_send.at[dz], f_recv.at[dz],
            device_id=other_core, device_id_type=MESH,
        )
        copy.start()
        if dz == 0:
            for to in WHOLE:
                for dc in range(NCORE):
                    pltpu.make_async_remote_copy(
                        pooled.at[at, :, core], pooled.at[at, :, core], n_send, p_recv.at[to],
                        device_id=offset(0, to, 0, dc), device_id_type=MESH,
                    ).start()
        return copy

    def products(dz):
        plane = lax.rem(z + NZ - dz, NZ)
        columns = pl.ds(pl.multiple_of(plane * ZCOLS, ZCOLS), ZCOLS)
        value = jnp.concatenate(
            [pooled[plane * NY + i].reshape(NDOC, LANES) for i in range(NY)], axis=1
        )
        high, low = split(value)
        gram[...] += nt_dot(
            jnp.concatenate([high, high, low], axis=1), jnp.concatenate([high, low, high], axis=1)
        )
        high, low = split(value * w_ref[:, columns])
        both = jnp.concatenate([high, low], axis=0)
        ww_ref[:, columns] = both
        for o in range(2):
            u[o] += nt_dot(hv[rows[o], :, columns], both)

    held = []
    for dz in TAKEN:
        copy = take(dz)
        if copy is not None:
            held.append((dz, copy))
            if len(held) < 2:
                continue
        while len(held) > (copy is not None):
            first, given = held.pop(0)
            given.wait()
            products(first)
        if copy is None:
            products(dz)
    for first, given in held:
        given.wait()
        products(first)

    k = lax.broadcasted_iota(jnp.int32, (NDOC, NDOC), 0)
    l = lax.broadcasted_iota(jnp.int32, (NDOC, NDOC), 1)
    eye = k == l
    table = gram[...]
    only = jnp.where(eye, table, 0.0)
    norm2 = jnp.sum(only, axis=1, keepdims=True) + EPS
    norms = jnp.sqrt(norm2) * jnp.sqrt(jnp.sum(only, axis=0, keepdims=True) + EPS)
    scaled = 1.0 / (norms * SHARPNESS)
    logits = table * scaled
    weights = jnp.where(eye, 0.0, jnp.exp(logits))
    sum_down = jnp.sum(weights, axis=1, keepdims=True)
    sum_along = jnp.sum(weights, axis=0, keepdims=True)
    pair = jnp.where(partner_ref[...] == k, 1.0, 0.0)
    target = jnp.sum(jnp.sum(pair * logits, axis=1, keepdims=True), axis=0, keepdims=True)
    logs = jnp.sum(jnp.log(sum_down), axis=0, keepdims=True)
    loss_ref[...] = (logs - target) * (1.0 / NDOC)
    change = (weights * (1.0 / sum_down + 1.0 / sum_along) - 2.0 * pair) * (1.0 / NDOC)
    own = jnp.sum(change * logits, axis=1, keepdims=True) / norm2
    sym[...] = change * scaled - jnp.where(eye, own, 0.0)

    place = (seq * TOK + lax.broadcasted_iota(jnp.int32, (TOK, 128), 0)).astype(F32)
    for o in range(2):
        lengths, _, _, start_along = bounds(len_ref, rows[o])
        ours = sym[pl.ds(pl.multiple_of((x * NCORE + rows[o]) * DOCS_ROW, DOCS_ROW), DOCS_ROW), :]
        ours = ours * (LOSS_SCALE / lengths)
        ours = jnp.concatenate([ours, ours], axis=1)
        mix = jnp.broadcast_to(ours[0:1], (TOK, 128))
        for d in range(1, DOCS_ROW):
            mix = jnp.where(place >= start_along[:, d : d + 1], ours[d : d + 1], mix)
        inner = jnp.sum(u[o] * mix, axis=1, keepdims=True) * (1.0 / D)
        inv = sb[o]
        a_ref[rows[o]] = inv * inv * inv * inner
        high, low = split(inv * mix)
        bb_ref[rows[o], :, 0:128] = high
        bb_ref[rows[o], :, 128:256] = low

    some = pl.ds(0, len(RELAYED))
    pltpu.make_async_copy(rs_in.at[some], rs_in.at[some], z_send).wait()
    for _ in range(2 * len(WHOLE)):
        some = pl.ds(0, PLANE)
        pltpu.make_async_copy(rs_in.at[some], rs_in.at[some], n_send).wait()
    left = sum(len(offsets(dz)) for dz in (0, *RELAYED))
    while left:
        some = pl.ds(0, min(left, CHIPS))
        pltpu.make_async_copy(rs_in.at[some], rs_in.at[some], p_send).wait()
        left -= min(left, CHIPS)


def grad_kernel(h_ref, bb_ref, a_ref, ww_ref, loss_ref, out_hbm, loss_out, out, sem):
    copies = [pltpu.make_async_copy(loss_ref, loss_out, sem.at[D // WIDTH])]
    copies[0].start()
    for n in range(D // WIDTH):
        columns = slice(n * WIDTH, (n + 1) * WIDTH)
        both = ww_ref[:, columns]
        both = jnp.concatenate([both, both], axis=0)
        for r in range(2):
            first = jnp.dot(bb_ref[r], both, preferred_element_type=F32)
            a = jnp.concatenate([a_ref[r]] * (WIDTH // 128), axis=1)
            out[r, :, columns] = (first - h_ref[r, :, columns].astype(F32) * a).astype(BF16)
        copy = pltpu.make_async_copy(out.at[:, :, columns], out_hbm.at[:, :, columns], sem.at[n])
        copy.start()
        copies.append(copy)
    for copy in copies:
        copy.wait()


def shards(hidden, doc_lengths, partner, closing_layer_weight):
    vmem = pl.BlockSpec(memory_space=pltpu.VMEM)
    hbm = pl.BlockSpec(memory_space=pltpu.HBM)
    dma = pltpu.SemaphoreType.DMA
    arguments = (hidden, doc_lengths, partner.reshape(1, NDOC), closing_layer_weight.reshape(1, D))
    h, bb, a, ww, loss = pl.pallas_call(
        pool_kernel,
        out_shape=(
            pltpu.VMEM((2, TOK, D), BF16),
            pltpu.VMEM((2, TOK, 256), BF16),
            pltpu.VMEM((2, TOK, 128), F32),
            pltpu.VMEM((2 * NDOC, D), BF16),
            pltpu.VMEM((1, 1), F32),
        ),
        in_specs=[hbm] * 4,
        out_specs=(vmem,) * 5,
        scratch_shapes=[
            pltpu.VMEM((2, DOCS_ROW), jnp.int32),
            pltpu.VMEM((1, NDOC), jnp.int32),
            pltpu.VMEM((1, D), F32),
            pltpu.VMEM((2, TOK, 128), F32),
            pltpu.VMEM((CHIPS, DOCS_ROW, LANES), F32),
            pltpu.VMEM((CHIPS, DOCS_ROW, LANES), F32),
            pltpu.VMEM((CHIPS, DOCS_ROW, LANES), F32),
            pltpu.VMEM((CHIPS, DOCS_ROW, LANES), F32),
            pltpu.VMEM((CHIPS, NX, NCORE, DOCS_ROW, LANES), F32),
            pltpu.VMEM((2, TOK, 128), F32),
            pltpu.VMEM((NDOC, NDOC), F32),
            pltpu.VMEM((NDOC, NDOC), F32),
            dma((2 * PARTS,)), dma((3,)),
            dma((PARTS,)), dma((PARTS,)),
            dma, dma,
            dma, dma((NZ,)),
            dma, dma((NZ,)),
            dma((NZ,)), dma((NZ,)),
            dma,
        ],
        compiler_params=pltpu.CompilerParams(
            collective_id=0, has_side_effects=True, vmem_limit_bytes=16 * 1024 * 1024
        ),
        name="pool_and_loss",
    )(*(pltpu.with_memory_space_constraint(v, pltpu.HBM) for v in arguments))
    out, loss = pl.pallas_call(
        grad_kernel,
        out_shape=(
            jax.ShapeDtypeStruct((2, TOK, D), BF16),
            jax.ShapeDtypeStruct((1, 1), F32),
        ),
        in_specs=[vmem] * 5,
        out_specs=(pl.BlockSpec(memory_space=pl.ANY),) * 2,
        scratch_shapes=[pltpu.VMEM((2, TOK, D), BF16), dma((D // WIDTH + 1,))],
        compiler_params=pltpu.CompilerParams(vmem_limit_bytes=16 * 1024 * 1024),
        name="hidden_gradient",
    )(h, bb, a, ww, loss)
    return out, loss.reshape(())


def solution(mesh):
    in_specs = (P("dp", "seq", None), P("dp", None), P(), P())
    out_specs = (P("dp", "seq", None), P())
    return jax.shard_map(shards, mesh=mesh, in_specs=in_specs, out_specs=out_specs, check_vma=False)
```

```python
import jax
import jax.numpy as jnp
from jax import lax
from jax.experimental import pallas as pl
from jax.experimental.pallas import tpu as pltpu
from jax.sharding import PartitionSpec as P

MESH = pl.DeviceIdType.MESH
F32, BF16 = jnp.float32, jnp.bfloat16

SHARPNESS = 0.05
LOSS_SCALE = 524288.0
EPS = 1e-06

NX, NZ, NY, NCORE = 4, 8, 4, 2
CHIPS = NZ * NY
PLANE = NX * NY
D = 4096
DOCS_ROW = 8
NDOC = 64
TOK = 256
LANES = D // CHIPS
ZCOLS = LANES * NY
PARTS = 4
WIDTHS = (256, 256, 512, 512, 512, 512, 512, 512, 256, 256)
BOTH = (4,)
WHOLE = (1, 7)
RELAYED = (2, 6, 3, 5, 4)
TAKEN = (0, 2, 6, 1, 7, 3, 5, 4)
IN_FLIGHT = 8


def offsets(dz):
    found = []
    for i in range(1, PLANE * NCORE):
        dx, dy, dc = i // (NY * NCORE), i // NCORE % NY, i % NCORE
        if dz in BOTH or dc == 0:
            found.append((dx, dy, dc))
    return sorted(found, key=lambda t: -min(t[0], NX - t[0]) - min(t[1], NY - t[1]))


def peers():
    found = [(dz, 0, dy, 0) for dz in range(1, NZ) for dy in range(NY)]
    found += [(0, *at) for at in offsets(BOTH[0])] + [(dz, 0, 0, 1) for dz in WHOLE]

    def hops(t):
        return min(t[0], NZ - t[0]) + min(t[1], NX - t[1]) + min(t[2], NY - t[2])

    return sorted(found, key=lambda t: -hops(t))


PEERS = peers()
NEXT = 16


def bounds(len_ref, row):
    along = len_ref[pl.ds(row, 1), :].astype(F32)
    k = lax.broadcasted_iota(jnp.int32, (DOCS_ROW, DOCS_ROW), 0)
    l = lax.broadcasted_iota(jnp.int32, (DOCS_ROW, DOCS_ROW), 1)
    spread = jnp.broadcast_to(along, (DOCS_ROW, DOCS_ROW))
    down = jnp.sum(jnp.where(k == l, spread, 0.0), axis=1, keepdims=True)
    finish_down = jnp.sum(jnp.where(l <= k, spread, 0.0), axis=1, keepdims=True)
    start_down = finish_down - down
    start_along = jnp.sum(jnp.where(k < l, jnp.broadcast_to(down, (DOCS_ROW, DOCS_ROW)), 0.0), axis=0, keepdims=True)
    return down, start_down, finish_down, start_along


def split(value):
    high = value.astype(BF16)
    return high, (value - high.astype(F32)).astype(BF16)


def nt_dot(a, b):
    return lax.dot_general(a, b, (((1,), (1,)), ((), ())), preferred_element_type=F32)


def pool_kernel(
    h_hbm, len_hbm, partner_hbm, w_hbm,
    hv, bb_ref, a_ref, ww_ref, loss_ref,
    len_ref, partner_ref, w_ref, sb, csend, crecv, rbuf, rs_in, pooled, u, gram, sym,
    load_sem, small_sem, core_send, core_recv, rs_send, rs_recv, z_send, z_recv, p_send, p_recv, f_send, f_recv, n_send,
):
    x = lax.axis_index("dp")
    seq = lax.axis_index("seq")
    chip = lax.div(seq, NCORE)
    core = lax.rem(seq, NCORE)
    z = lax.div(chip, NY)
    y = lax.rem(chip, NY)
    rows = (1 - core, core)

    def device(to_x, to_chip, to_core=core):
        return (to_x, to_chip * NCORE + to_core)

    def offset(dx, dz, dy, dc=None):
        return device(
            lax.rem(x + dx, NX),
            lax.rem(z + dz, NZ) * NY + lax.rem(y + dy, NY),
            lax.rem(core + dc, NCORE) if dc is not None else core,
        )

    other_core = (x, chip * NCORE + 1 - core)

    barrier = pltpu.get_barrier_semaphore()

    def greet(to):
        pl.semaphore_signal(barrier, inc=1, device_id=to, device_id_type=MESH)

    for dz, dx, dy, dc in PEERS[:NEXT]:
        greet(offset(dx, dz, dy, dc))

    small = []
    for n, (here, there) in enumerate(
        ((len_hbm, len_ref), (w_hbm, w_ref), (partner_hbm, partner_ref))
    ):
        copy = pltpu.make_async_copy(here, there, small_sem.at[n])
        copy.start()
        small.append(copy)
    loads = []
    for o in range(2):
        for q in range(PARTS):
            part = pl.ds(q * (TOK // PARTS), TOK // PARTS)
            copy = pltpu.make_async_copy(
                h_hbm.at[rows[o], part], hv.at[rows[o], part], load_sem.at[o * PARTS + q]
            )
            loads.append(copy)
    for copy in loads[:IN_FLIGHT]:
        copy.start()

    for dz, dx, dy, dc in PEERS[NEXT:]:
        greet(offset(dx, dz, dy, dc))

    def squares(o, q):
        n = o * PARTS + q
        loads[n].wait()
        if n + IN_FLIGHT < len(loads):
            loads[n + IN_FLIGHT].start()
        at = pl.ds(q * (TOK // PARTS), TOK // PARTS)
        acc = jnp.zeros((TOK // PARTS, 128), F32)
        for t in range(D // 128):
            v = hv[rows[o], at, t * 128 : (t + 1) * 128].astype(F32)
            acc = acc + v * v
        sb[o, at, :] = acc

    along = (seq * TOK + lax.broadcasted_iota(jnp.int32, (DOCS_ROW, TOK), 1)).astype(F32)

    def selector(o):
        _, start_down, finish_down, _ = bounds(len_ref, rows[o])
        inv = lax.rsqrt(jnp.sum(sb[o].T, axis=0, keepdims=True) * (1.0 / D) + EPS)
        member = (along >= start_down) & (along < finish_down)
        high, low = split(jnp.where(member, inv, 0.0))
        return jnp.concatenate([high, low], axis=0)

    def sums(chosen, o, part):
        columns = pl.ds(pl.multiple_of(part * (D // PARTS), D // PARTS), D // PARTS)
        both = jnp.dot(chosen, hv[rows[o], :, columns], preferred_element_type=F32)
        return both[0:DOCS_ROW] + both[DOCS_ROW : 2 * DOCS_ROW]

    per_part = CHIPS // PARTS
    order = [lax.rem(lax.div(z * PARTS, NZ) + n, PARTS) for n in (2, 1, 3, 0)]
    for q in range(PARTS):
        squares(0, q)
    for copy in small:
        copy.wait()
    chosen = selector(0)
    for part in order:
        value = sums(chosen, 0, part)
        for b in range(per_part):
            csend[part * per_part + b] = value[:, b * LANES : (b + 1) * LANES]
    for q in range(PARTS):
        squares(1, q)
    chosen = selector(1)
    for part in order:
        value = sums(chosen, 1, part)
        for b in range(per_part):
            rbuf[part * per_part + b] = value[:, b * LANES : (b + 1) * LANES]
    pl.semaphore_wait(barrier, len(PEERS))
    core_copies = []
    for q, part in enumerate(order):
        at = pl.ds(part * per_part, per_part)
        copy = pltpu.make_async_remote_copy(
            csend.at[at], crecv.at[at], core_send.at[q], core_recv.at[q],
            device_id=other_core, device_id_type=MESH,
        )
        copy.start()
        core_copies.append(copy)
    for q, part in enumerate(order):
        core_copies[q].wait_recv()
        at = pl.ds(part * per_part, per_part)
        rbuf[at] = rbuf[at] + crecv[at]
        for b in range(per_part):
            to = part * per_part + b

            def scatter(to=to):
                pltpu.make_async_remote_copy(
                    rbuf.at[to], rs_in.at[chip], rs_send, rs_recv,
                    device_id=device(x, to), device_id_type=MESH,
                ).start()

            if q + 1 < PARTS:
                scatter()
            else:
                pl.when(to != chip)(scatter)
    for copy in core_copies:
        copy.wait_send()

    rs_in[pl.ds(chip, 1)] = rbuf[pl.ds(chip, 1)]
    for o in range(2):
        square = jnp.sum(sb[o], axis=1, keepdims=True) * (1.0 / D)
        sb[o] = jnp.broadcast_to(lax.rsqrt(square + EPS), (TOK, 128))
    u[...] = jnp.zeros_like(u)
    gram[...] = jnp.zeros_like(gram)
    lengths, _, _, _ = bounds(len_ref, core)
    pltpu.make_async_remote_copy(
        rbuf.at[pl.ds(0, CHIPS - 1)], rs_in.at[pl.ds(0, CHIPS - 1)], rs_send, rs_recv,
        device_id=other_core, device_id_type=MESH,
    ).wait()
    total = jnp.sum(rs_in[...], axis=0)
    gain = w_ref[:, pl.ds(pl.multiple_of(chip * LANES, LANES), LANES)]
    pooled[chip, x, core] = total * gain / lengths

    mine = pooled.at[chip, x, core]

    def passed(dz):
        return pooled.at[lax.rem(z + NZ - dz, NZ) * NY + y, x, core]

    def send(tile, dz, to):
        pltpu.make_async_remote_copy(
            tile, tile, p_send, p_recv.at[dz], device_id=to, device_id_type=MESH
        ).start()

    def to_plane(dz):
        tile = passed(dz)
        for dx, dy, dc in offsets(dz):
            send(tile, dz, offset(dx, 0, dy, dc))

    for dz in RELAYED[::-1]:
        pltpu.make_async_remote_copy(
            mine, mine, z_send, z_recv.at[dz], device_id=offset(0, dz, 0), device_id_type=MESH
        ).start()
    to_plane(0)
    for dz in RELAYED:
        tile = passed(dz)
        pltpu.make_async_remote_copy(
            tile, tile, z_send, z_recv.at[dz], device_id=other_core, device_id_type=MESH
        ).wait_recv()
        to_plane(dz)

    def take(dz):
        parts = PLANE * NCORE if dz in WHOLE else PLANE * NCORE - 1 if dz in BOTH else PLANE - 1
        got = pl.ds(0, parts)
        pltpu.make_async_remote_copy(
            rs_in.at[got], rs_in.at[got], p_send, p_recv.at[dz],
            device_id=other_core, device_id_type=MESH,
        ).wait_recv()
        if dz in BOTH or dz in WHOLE:
            return None
        at = pl.ds(lax.rem(z + NZ - dz, NZ) * NY, NY)
        copy = pltpu.make_async_remote_copy(
            pooled.at[at, :, core], pooled.at[at, :, core], f_send.at[dz], f_recv.at[dz],
            device_id=other_core, device_id_type=MESH,
        )
        copy.start()
        if dz == 0:
            for to in WHOLE:
                for dc in range(NCORE):
                    pltpu.make_async_remote_copy(
                        pooled.at[at, :, core], pooled.at[at, :, core], n_send, p_recv.at[to],
                        device_id=offset(0, to, 0, dc), device_id_type=MESH,
                    ).start()
        return copy

    def products(dz, last=False):
        plane = lax.rem(z + NZ - dz, NZ)
        columns = pl.ds(pl.multiple_of(plane * ZCOLS, ZCOLS), ZCOLS)
        value = jnp.concatenate(
            [pooled[plane * NY + i].reshape(NDOC, LANES) for i in range(NY)], axis=1
        )
        high, low = split(value)
        gram[...] += nt_dot(
            jnp.concatenate([high, high, low], axis=1), jnp.concatenate([high, low, high], axis=1)
        )
        high, low = split(value * w_ref[:, columns])
        both = jnp.concatenate([high, low], axis=0)

        def inner():
            ww_ref[:, columns] = both
            for o in range(2):
                u[o] += nt_dot(hv[rows[o], :, columns], both)

        if last:
            return inner
        inner()

    held = []
    for dz in TAKEN:
        copy = take(dz)
        if copy is not None:
            held.append((dz, copy))
            if len(held) < 2:
                continue
        while len(held) > (copy is not None):
            first, given = held.pop(0)
            given.wait()
            products(first)
        if copy is None:
            rest = products(dz, dz == TAKEN[-1])

    k = lax.broadcasted_iota(jnp.int32, (NDOC, NDOC), 0)
    l = lax.broadcasted_iota(jnp.int32, (NDOC, NDOC), 1)
    eye = k == l
    table = gram[...]
    only = jnp.where(eye, table, 0.0)
    norm2 = jnp.sum(only, axis=1, keepdims=True) + EPS
    norms = jnp.sqrt(norm2) * jnp.sqrt(jnp.sum(only, axis=0, keepdims=True) + EPS)
    scaled = 1.0 / (norms * SHARPNESS)
    logits = table * scaled
    weights = jnp.where(eye, 0.0, jnp.exp(logits))
    sum_down = jnp.sum(weights, axis=1, keepdims=True)
    sum_along = jnp.sum(weights, axis=0, keepdims=True)
    pair = jnp.where(partner_ref[...] == k, 1.0, 0.0)
    target = jnp.sum(jnp.sum(pair * logits, axis=1, keepdims=True), axis=0, keepdims=True)
    logs = jnp.sum(jnp.log(sum_down), axis=0, keepdims=True)
    loss_ref[...] = (logs - target) * (1.0 / NDOC)
    change = (weights * (1.0 / sum_down + 1.0 / sum_along) - 2.0 * pair) * (1.0 / NDOC)
    own = jnp.sum(change * logits, axis=1, keepdims=True) / norm2
    sym[...] = change * scaled - jnp.where(eye, own, 0.0)

    rest()

    place = (seq * TOK + lax.broadcasted_iota(jnp.int32, (TOK, 128), 0)).astype(F32)
    for o in range(2):
        lengths, _, _, start_along = bounds(len_ref, rows[o])
        ours = sym[pl.ds(pl.multiple_of((x * NCORE + rows[o]) * DOCS_ROW, DOCS_ROW), DOCS_ROW), :]
        ours = ours * (LOSS_SCALE / lengths)
        ours = jnp.concatenate([ours, ours], axis=1)
        mix = jnp.broadcast_to(ours[0:1], (TOK, 128))
        for d in range(1, DOCS_ROW):
            mix = jnp.where(place >= start_along[:, d : d + 1], ours[d : d + 1], mix)
        inner = jnp.sum(u[o] * mix, axis=1, keepdims=True) * (1.0 / D)
        inv = sb[o]
        a_ref[rows[o]] = inv * inv * inv * inner
        high, low = split(inv * mix)
        bb_ref[rows[o], :, 0:128] = high
        bb_ref[rows[o], :, 128:256] = low

    some = pl.ds(0, len(RELAYED))
    pltpu.make_async_copy(rs_in.at[some], rs_in.at[some], z_send).wait()
    for _ in range(2 * len(WHOLE)):
        some = pl.ds(0, PLANE)
        pltpu.make_async_copy(rs_in.at[some], rs_in.at[some], n_send).wait()
    left = sum(len(offsets(dz)) for dz in (0, *RELAYED))
    while left:
        some = pl.ds(0, min(left, CHIPS))
        pltpu.make_async_copy(rs_in.at[some], rs_in.at[some], p_send).wait()
        left -= min(left, CHIPS)


def grad_kernel(h_ref, bb_ref, a_ref, ww_ref, loss_ref, out_hbm, loss_out, out, sem):
    copies = [pltpu.make_async_copy(loss_ref, loss_out, sem.at[len(WIDTHS)])]
    copies[0].start()
    for n, width in enumerate(WIDTHS):
        columns = slice(sum(WIDTHS[:n]), sum(WIDTHS[: n + 1]))
        both = ww_ref[:, columns]
        both = jnp.concatenate([both, both], axis=0)
        for r in range(2):
            first = jnp.dot(bb_ref[r], both, preferred_element_type=F32)
            a = jnp.concatenate([a_ref[r]] * (width // 128), axis=1)
            out[r, :, columns] = (first - h_ref[r, :, columns].astype(F32) * a).astype(BF16)
        copy = pltpu.make_async_copy(out.at[:, :, columns], out_hbm.at[:, :, columns], sem.at[n])
        copy.start()
        copies.append(copy)
    for copy in copies:
        copy.wait()


def shards(hidden, doc_lengths, partner, closing_layer_weight):
    vmem = pl.BlockSpec(memory_space=pltpu.VMEM)
    hbm = pl.BlockSpec(memory_space=pltpu.HBM)
    dma = pltpu.SemaphoreType.DMA
    arguments = (hidden, doc_lengths, partner.reshape(1, NDOC), closing_layer_weight.reshape(1, D))
    h, bb, a, ww, loss = pl.pallas_call(
        pool_kernel,
        out_shape=(
            pltpu.VMEM((2, TOK, D), BF16),
            pltpu.VMEM((2, TOK, 256), BF16),
            pltpu.VMEM((2, TOK, 128), F32),
            pltpu.VMEM((2 * NDOC, D), BF16),
            pltpu.VMEM((1, 1), F32),
        ),
        in_specs=[hbm] * 4,
        out_specs=(vmem,) * 5,
        scratch_shapes=[
            pltpu.VMEM((2, DOCS_ROW), jnp.int32),
            pltpu.VMEM((1, NDOC), jnp.int32),
            pltpu.VMEM((1, D), F32),
            pltpu.VMEM((2, TOK, 128), F32),
            pltpu.VMEM((CHIPS, DOCS_ROW, LANES), F32),
            pltpu.VMEM((CHIPS, DOCS_ROW, LANES), F32),
            pltpu.VMEM((CHIPS, DOCS_ROW, LANES), F32),
            pltpu.VMEM((CHIPS, DOCS_ROW, LANES), F32),
            pltpu.VMEM((CHIPS, NX, NCORE, DOCS_ROW, LANES), F32),
            pltpu.VMEM((2, TOK, 128), F32),
            pltpu.VMEM((NDOC, NDOC), F32),
            pltpu.VMEM((NDOC, NDOC), F32),
            dma((2 * PARTS,)), dma((3,)),
            dma((PARTS,)), dma((PARTS,)),
            dma, dma,
            dma, dma((NZ,)),
            dma, dma((NZ,)),
            dma((NZ,)), dma((NZ,)),
            dma,
        ],
        compiler_params=pltpu.CompilerParams(
            collective_id=0, has_side_effects=True, vmem_limit_bytes=16 * 1024 * 1024
        ),
        name="pool_and_loss",
    )(*(pltpu.with_memory_space_constraint(v, pltpu.HBM) for v in arguments))
    out, loss = pl.pallas_call(
        grad_kernel,
        out_shape=(
            jax.ShapeDtypeStruct((2, TOK, D), BF16),
            jax.ShapeDtypeStruct((1, 1), F32),
        ),
        in_specs=[vmem] * 5,
        out_specs=(pl.BlockSpec(memory_space=pl.ANY),) * 2,
        scratch_shapes=[pltpu.VMEM((2, TOK, D), BF16), dma((len(WIDTHS) + 1,))],
        compiler_params=pltpu.CompilerParams(vmem_limit_bytes=16 * 1024 * 1024),
        name="hidden_gradient",
    )(h, bb, a, ww, loss)
    return out, loss.reshape(())


def solution(mesh):
    in_specs = (P("dp", "seq", None), P("dp", None), P(), P())
    out_specs = (P("dp", "seq", None), P())
    return jax.shard_map(shards, mesh=mesh, in_specs=in_specs, out_specs=out_specs, check_vma=False)
```

```python
import jax
import jax.numpy as jnp
from jax import lax
from jax.experimental import pallas as pl
from jax.experimental.pallas import tpu as pltpu
from jax.sharding import PartitionSpec as P

MESH = pl.DeviceIdType.MESH
F32, BF16 = jnp.float32, jnp.bfloat16

SHARPNESS = 0.05
LOSS_SCALE = 524288.0
EPS = 1e-06

NX, NZ, NY, NCORE = 4, 8, 4, 2
CHIPS = NZ * NY
PLANE = NX * NY
D = 4096
DOCS_ROW = 8
NDOC = 64
TOK = 256
LANES = D // CHIPS
ZCOLS = LANES * NY
PARTS = 4
WIDTHS = (256, 256, 512, 512, 512, 512, 512, 512, 256, 256)
BOTH = (4,)
WHOLE = (1, 7)
RELAYED = (2, 6, 3, 5, 4)
TAKEN = (0, 2, 6, 1, 7, 3, 5, 4)
IN_FLIGHT = 8


def offsets(dz):
    found = []
    for i in range(1, PLANE * NCORE):
        dx, dy, dc = i // (NY * NCORE), i // NCORE % NY, i % NCORE
        if dz in BOTH or dc == 0:
            found.append((dx, dy, dc))
    return sorted(found, key=lambda t: -min(t[0], NX - t[0]) - min(t[1], NY - t[1]))


def peers():
    found = [(dz, 0, dy, 0) for dz in range(1, NZ) for dy in range(NY)]
    found += [(0, *at) for at in offsets(BOTH[0])] + [(dz, 0, 0, 1) for dz in WHOLE]

    def hops(t):
        return min(t[0], NZ - t[0]) + min(t[1], NX - t[1]) + min(t[2], NY - t[2])

    return sorted(found, key=lambda t: -hops(t))


PEERS = peers()
NEXT = 16


def bounds(len_ref, row):
    along = len_ref[pl.ds(row, 1), :].astype(F32)
    k = lax.broadcasted_iota(jnp.int32, (DOCS_ROW, DOCS_ROW), 0)
    l = lax.broadcasted_iota(jnp.int32, (DOCS_ROW, DOCS_ROW), 1)
    spread = jnp.broadcast_to(along, (DOCS_ROW, DOCS_ROW))
    down = jnp.sum(jnp.where(k == l, spread, 0.0), axis=1, keepdims=True)
    finish_down = jnp.sum(jnp.where(l <= k, spread, 0.0), axis=1, keepdims=True)
    start_down = finish_down - down
    start_along = jnp.sum(jnp.where(k < l, jnp.broadcast_to(down, (DOCS_ROW, DOCS_ROW)), 0.0), axis=0, keepdims=True)
    return down, start_down, finish_down, start_along


def split(value):
    high = value.astype(BF16)
    return high, (value - high.astype(F32)).astype(BF16)


def nt_dot(a, b):
    return lax.dot_general(a, b, (((1,), (1,)), ((), ())), preferred_element_type=F32)


def pool_kernel(
    h_hbm, len_hbm, partner_hbm, w_hbm,
    hv, bb_ref, a_ref, ww_ref, loss_ref,
    len_ref, partner_ref, w_ref, sb, csend, crecv, rbuf, rs_in, pooled, u, gram, sym,
    load_sem, small_sem, core_send, core_recv, rs_send, rs_recv, z_send, z_recv, p_send, p_recv, f_send, f_recv, n_send,
):
    x = lax.axis_index("dp")
    seq = lax.axis_index("seq")
    chip = lax.div(seq, NCORE)
    core = lax.rem(seq, NCORE)
    z = lax.div(chip, NY)
    y = lax.rem(chip, NY)
    rows = (1 - core, core)

    def device(to_x, to_chip, to_core=core):
        return (to_x, to_chip * NCORE + to_core)

    def offset(dx, dz, dy, dc=None):
        return device(
            lax.rem(x + dx, NX),
            lax.rem(z + dz, NZ) * NY + lax.rem(y + dy, NY),
            lax.rem(core + dc, NCORE) if dc is not None else core,
        )

    other_core = (x, chip * NCORE + 1 - core)

    barrier = pltpu.get_barrier_semaphore()

    def greet(to):
        pl.semaphore_signal(barrier, inc=1, device_id=to, device_id_type=MESH)

    for dz, dx, dy, dc in PEERS[:NEXT]:
        greet(offset(dx, dz, dy, dc))

    small = []
    for n, (here, there) in enumerate(
        ((len_hbm, len_ref), (w_hbm, w_ref), (partner_hbm, partner_ref))
    ):
        copy = pltpu.make_async_copy(here, there, small_sem.at[n])
        copy.start()
        small.append(copy)
    loads = []
    for o in range(2):
        for q in range(PARTS):
            part = pl.ds(q * (TOK // PARTS), TOK // PARTS)
            copy = pltpu.make_async_copy(
                h_hbm.at[rows[o], part], hv.at[rows[o], part], load_sem.at[o * PARTS + q]
            )
            loads.append(copy)
    for copy in loads[:IN_FLIGHT]:
        copy.start()

    for dz, dx, dy, dc in PEERS[NEXT:]:
        greet(offset(dx, dz, dy, dc))

    def squares(o, q):
        n = o * PARTS + q
        loads[n].wait()
        if n + IN_FLIGHT < len(loads):
            loads[n + IN_FLIGHT].start()
        at = pl.ds(q * (TOK // PARTS), TOK // PARTS)
        acc = jnp.zeros((TOK // PARTS, 128), F32)
        for t in range(D // 128):
            v = hv[rows[o], at, t * 128 : (t + 1) * 128].astype(F32)
            acc = acc + v * v
        sb[o, at, :] = acc

    along = (seq * TOK + lax.broadcasted_iota(jnp.int32, (DOCS_ROW, TOK), 1)).astype(F32)

    def selector(o):
        _, start_down, finish_down, _ = bounds(len_ref, rows[o])
        inv = lax.rsqrt(jnp.sum(sb[o].T, axis=0, keepdims=True) * (1.0 / D) + EPS)
        member = (along >= start_down) & (along < finish_down)
        high, low = split(jnp.where(member, inv, 0.0))
        return jnp.concatenate([high, low], axis=0)

    def sums(chosen, o, part):
        columns = pl.ds(pl.multiple_of(part * (D // PARTS), D // PARTS), D // PARTS)
        both = jnp.dot(chosen, hv[rows[o], :, columns], preferred_element_type=F32)
        return both[0:DOCS_ROW] + both[DOCS_ROW : 2 * DOCS_ROW]

    per_part = CHIPS // PARTS
    order = [lax.rem(lax.div(z * PARTS, NZ) + n, PARTS) for n in (2, 1, 3, 0)]
    for q in range(PARTS):
        squares(0, q)
    for copy in small:
        copy.wait()
    chosen = selector(0)
    for part in order:
        value = sums(chosen, 0, part)
        for b in range(per_part):
            csend[part * per_part + b] = value[:, b * LANES : (b + 1) * LANES]
    for q in range(PARTS):
        squares(1, q)
    chosen = selector(1)
    for part in order:
        value = sums(chosen, 1, part)
        for b in range(per_part):
            rbuf[part * per_part + b] = value[:, b * LANES : (b + 1) * LANES]
    pl.semaphore_wait(barrier, len(PEERS))
    core_copies = []
    for q, part in enumerate(order):
        at = pl.ds(part * per_part, per_part)
        copy = pltpu.make_async_remote_copy(
            csend.at[at], crecv.at[at], core_send.at[q], core_recv.at[q],
            device_id=other_core, device_id_type=MESH,
        )
        copy.start()
        core_copies.append(copy)
    for q, part in enumerate(order):
        core_copies[q].wait_recv()
        at = pl.ds(part * per_part, per_part)
        rbuf[at] = rbuf[at] + crecv[at]
        for b in range(per_part):
            along_y = lax.rem(y + (2, 1, 3, 0)[b // (NZ // PARTS)], NY)
            to = part * per_part + b % (NZ // PARTS) * NY + along_y

            def scatter(to=to):
                pltpu.make_async_remote_copy(
                    rbuf.at[to], rs_in.at[chip], rs_send, rs_recv,
                    device_id=device(x, to), device_id_type=MESH,
                ).start()

            if q + 1 < PARTS:
                scatter()
            else:
                pl.when(to != chip)(scatter)
    for copy in core_copies:
        copy.wait_send()

    rs_in[pl.ds(chip, 1)] = rbuf[pl.ds(chip, 1)]
    for o in range(2):
        square = jnp.sum(sb[o], axis=1, keepdims=True) * (1.0 / D)
        sb[o] = jnp.broadcast_to(lax.rsqrt(square + EPS), (TOK, 128))
    u[...] = jnp.zeros_like(u)
    gram[...] = jnp.zeros_like(gram)
    lengths, _, _, _ = bounds(len_ref, core)
    pltpu.make_async_remote_copy(
        rbuf.at[pl.ds(0, CHIPS - 1)], rs_in.at[pl.ds(0, CHIPS - 1)], rs_send, rs_recv,
        device_id=other_core, device_id_type=MESH,
    ).wait()
    total = jnp.sum(rs_in[...], axis=0)
    gain = w_ref[:, pl.ds(pl.multiple_of(chip * LANES, LANES), LANES)]
    pooled[chip, x, core] = total * gain / lengths

    mine = pooled.at[chip, x, core]

    def passed(dz):
        return pooled.at[lax.rem(z + NZ - dz, NZ) * NY + y, x, core]

    def send(tile, dz, to):
        pltpu.make_async_remote_copy(
            tile, tile, p_send, p_recv.at[dz], device_id=to, device_id_type=MESH
        ).start()

    def to_plane(dz):
        tile = passed(dz)
        for dx, dy, dc in offsets(dz):
            send(tile, dz, offset(dx, 0, dy, dc))

    for dz in RELAYED[::-1]:
        pltpu.make_async_remote_copy(
            mine, mine, z_send, z_recv.at[dz], device_id=offset(0, dz, 0), device_id_type=MESH
        ).start()
    to_plane(0)
    for dz in RELAYED:
        tile = passed(dz)
        pltpu.make_async_remote_copy(
            tile, tile, z_send, z_recv.at[dz], device_id=other_core, device_id_type=MESH
        ).wait_recv()
        to_plane(dz)

    def take(dz):
        parts = PLANE * NCORE if dz in WHOLE else PLANE * NCORE - 1 if dz in BOTH else PLANE - 1
        got = pl.ds(0, parts)
        pltpu.make_async_remote_copy(
            rs_in.at[got], rs_in.at[got], p_send, p_recv.at[dz],
            device_id=other_core, device_id_type=MESH,
        ).wait_recv()
        if dz in BOTH or dz in WHOLE:
            return None
        at = pl.ds(lax.rem(z + NZ - dz, NZ) * NY, NY)
        copy = pltpu.make_async_remote_copy(
            pooled.at[at, :, core], pooled.at[at, :, core], f_send.at[dz], f_recv.at[dz],
            device_id=other_core, device_id_type=MESH,
        )
        copy.start()
        if dz == 0:
            for to in WHOLE:
                for dc in range(NCORE):
                    pltpu.make_async_remote_copy(
                        pooled.at[at, :, core], pooled.at[at, :, core], n_send, p_recv.at[to],
                        device_id=offset(0, to, 0, dc), device_id_type=MESH,
                    ).start()
        return copy

    def products(dz, last=False):
        plane = lax.rem(z + NZ - dz, NZ)
        columns = pl.ds(pl.multiple_of(plane * ZCOLS, ZCOLS), ZCOLS)
        value = jnp.concatenate(
            [pooled[plane * NY + i].reshape(NDOC, LANES) for i in range(NY)], axis=1
        )
        high, low = split(value)
        gram[...] += nt_dot(
            jnp.concatenate([high, high, low], axis=1), jnp.concatenate([high, low, high], axis=1)
        )
        high, low = split(value * w_ref[:, columns])
        both = jnp.concatenate([high, low], axis=0)

        def inner():
            ww_ref[:, columns] = both
            for o in range(2):
                u[o] += nt_dot(hv[rows[o], :, columns], both)

        if last:
            return inner
        inner()

    held = []
    for dz in TAKEN:
        copy = take(dz)
        if copy is not None:
            held.append((dz, copy))
            if len(held) < 2:
                continue
        while len(held) > (copy is not None):
            first, given = held.pop(0)
            given.wait()
            products(first)
        if copy is None:
            rest = products(dz, dz == TAKEN[-1])

    k = lax.broadcasted_iota(jnp.int32, (NDOC, NDOC), 0)
    l = lax.broadcasted_iota(jnp.int32, (NDOC, NDOC), 1)
    eye = k == l
    table = gram[...]
    only = jnp.where(eye, table, 0.0)
    norm2 = jnp.sum(only, axis=1, keepdims=True) + EPS
    norms = jnp.sqrt(norm2) * jnp.sqrt(jnp.sum(only, axis=0, keepdims=True) + EPS)
    scaled = 1.0 / (norms * SHARPNESS)
    logits = table * scaled
    weights = jnp.where(eye, 0.0, jnp.exp(logits))
    sum_down = jnp.sum(weights, axis=1, keepdims=True)
    sum_along = jnp.sum(weights, axis=0, keepdims=True)
    pair = jnp.where(partner_ref[...] == k, 1.0, 0.0)
    target = jnp.sum(jnp.sum(pair * logits, axis=1, keepdims=True), axis=0, keepdims=True)
    logs = jnp.sum(jnp.log(sum_down), axis=0, keepdims=True)
    loss_ref[...] = (logs - target) * (1.0 / NDOC)
    change = (weights * (1.0 / sum_down + 1.0 / sum_along) - 2.0 * pair) * (1.0 / NDOC)
    own = jnp.sum(change * logits, axis=1, keepdims=True) / norm2
    sym[...] = change * scaled - jnp.where(eye, own, 0.0)

    rest()

    place = (seq * TOK + lax.broadcasted_iota(jnp.int32, (TOK, 128), 0)).astype(F32)
    for o in range(2):
        lengths, _, _, start_along = bounds(len_ref, rows[o])
        ours = sym[pl.ds(pl.multiple_of((x * NCORE + rows[o]) * DOCS_ROW, DOCS_ROW), DOCS_ROW), :]
        ours = ours * (LOSS_SCALE / lengths)
        ours = jnp.concatenate([ours, ours], axis=1)
        mix = jnp.broadcast_to(ours[0:1], (TOK, 128))
        for d in range(1, DOCS_ROW):
            mix = jnp.where(place >= start_along[:, d : d + 1], ours[d : d + 1], mix)
        inner = jnp.sum(u[o] * mix, axis=1, keepdims=True) * (1.0 / D)
        inv = sb[o]
        a_ref[rows[o]] = inv * inv * inv * inner
        high, low = split(inv * mix)
        bb_ref[rows[o], :, 0:128] = high
        bb_ref[rows[o], :, 128:256] = low

    some = pl.ds(0, len(RELAYED))
    pltpu.make_async_copy(rs_in.at[some], rs_in.at[some], z_send).wait()
    for _ in range(2 * len(WHOLE)):
        some = pl.ds(0, PLANE)
        pltpu.make_async_copy(rs_in.at[some], rs_in.at[some], n_send).wait()
    left = sum(len(offsets(dz)) for dz in (0, *RELAYED))
    while left:
        some = pl.ds(0, min(left, CHIPS))
        pltpu.make_async_copy(rs_in.at[some], rs_in.at[some], p_send).wait()
        left -= min(left, CHIPS)


def grad_kernel(h_ref, bb_ref, a_ref, ww_ref, loss_ref, out_hbm, loss_out, out, sem):
    copies = [pltpu.make_async_copy(loss_ref, loss_out, sem.at[len(WIDTHS)])]
    copies[0].start()
    for n, width in enumerate(WIDTHS):
        columns = slice(sum(WIDTHS[:n]), sum(WIDTHS[: n + 1]))
        both = ww_ref[:, columns]
        both = jnp.concatenate([both, both], axis=0)
        for r in range(2):
            first = jnp.dot(bb_ref[r], both, preferred_element_type=F32)
            a = jnp.concatenate([a_ref[r]] * (width // 128), axis=1)
            out[r, :, columns] = (first - h_ref[r, :, columns].astype(F32) * a).astype(BF16)
        copy = pltpu.make_async_copy(out.at[:, :, columns], out_hbm.at[:, :, columns], sem.at[n])
        copy.start()
        copies.append(copy)
    for copy in copies:
        copy.wait()


def shards(hidden, doc_lengths, partner, closing_layer_weight):
    vmem = pl.BlockSpec(memory_space=pltpu.VMEM)
    hbm = pl.BlockSpec(memory_space=pltpu.HBM)
    dma = pltpu.SemaphoreType.DMA
    arguments = (hidden, doc_lengths, partner.reshape(1, NDOC), closing_layer_weight.reshape(1, D))
    h, bb, a, ww, loss = pl.pallas_call(
        pool_kernel,
        out_shape=(
            pltpu.VMEM((2, TOK, D), BF16),
            pltpu.VMEM((2, TOK, 256), BF16),
            pltpu.VMEM((2, TOK, 128), F32),
            pltpu.VMEM((2 * NDOC, D), BF16),
            pltpu.VMEM((1, 1), F32),
        ),
        in_specs=[hbm] * 4,
        out_specs=(vmem,) * 5,
        scratch_shapes=[
            pltpu.VMEM((2, DOCS_ROW), jnp.int32),
            pltpu.VMEM((1, NDOC), jnp.int32),
            pltpu.VMEM((1, D), F32),
            pltpu.VMEM((2, TOK, 128), F32),
            pltpu.VMEM((CHIPS, DOCS_ROW, LANES), F32),
            pltpu.VMEM((CHIPS, DOCS_ROW, LANES), F32),
            pltpu.VMEM((CHIPS, DOCS_ROW, LANES), F32),
            pltpu.VMEM((CHIPS, DOCS_ROW, LANES), F32),
            pltpu.VMEM((CHIPS, NX, NCORE, DOCS_ROW, LANES), F32),
            pltpu.VMEM((2, TOK, 128), F32),
            pltpu.VMEM((NDOC, NDOC), F32),
            pltpu.VMEM((NDOC, NDOC), F32),
            dma((2 * PARTS,)), dma((3,)),
            dma((PARTS,)), dma((PARTS,)),
            dma, dma,
            dma, dma((NZ,)),
            dma, dma((NZ,)),
            dma((NZ,)), dma((NZ,)),
            dma,
        ],
        compiler_params=pltpu.CompilerParams(
            collective_id=0, has_side_effects=True, vmem_limit_bytes=16 * 1024 * 1024
        ),
        name="pool_and_loss",
    )(*(pltpu.with_memory_space_constraint(v, pltpu.HBM) for v in arguments))
    out, loss = pl.pallas_call(
        grad_kernel,
        out_shape=(
            jax.ShapeDtypeStruct((2, TOK, D), BF16),
            jax.ShapeDtypeStruct((1, 1), F32),
        ),
        in_specs=[vmem] * 5,
        out_specs=(pl.BlockSpec(memory_space=pl.ANY),) * 2,
        scratch_shapes=[pltpu.VMEM((2, TOK, D), BF16), dma((len(WIDTHS) + 1,))],
        compiler_params=pltpu.CompilerParams(vmem_limit_bytes=16 * 1024 * 1024),
        name="hidden_gradient",
    )(h, bb, a, ww, loss)
    return out, loss.reshape(())


def solution(mesh):
    in_specs = (P("dp", "seq", None), P("dp", None), P(), P())
    out_specs = (P("dp", "seq", None), P())
    return jax.shard_map(shards, mesh=mesh, in_specs=in_specs, out_specs=out_specs, check_vma=False)
```

```python
import jax
import jax.numpy as jnp
from jax import lax
from jax.experimental import pallas as pl
from jax.experimental.pallas import tpu as pltpu
from jax.sharding import PartitionSpec as P

MESH = pl.DeviceIdType.MESH
F32, BF16 = jnp.float32, jnp.bfloat16

SHARPNESS = 0.05
LOSS_SCALE = 524288.0
EPS = 1e-06

NX, NZ, NY, NCORE = 4, 8, 4, 2
CHIPS = NZ * NY
PLANE = NX * NY
D = 4096
DOCS_ROW = 8
NDOC = 64
TOK = 256
LANES = D // CHIPS
ZCOLS = LANES * NY
PARTS = 4
WIDTHS = (256, 256, 512, 512, 512, 512, 512, 512, 256, 256)
BOTH = (4,)
WHOLE = (1, 7)
RELAYED = (2, 6, 3, 5, 4)
TAKEN = (0, 2, 6, 1, 7, 3, 5, 4)
IN_FLIGHT = 8


def offsets(dz):
    found = []
    for i in range(1, PLANE * NCORE):
        dx, dy, dc = i // (NY * NCORE), i // NCORE % NY, i % NCORE
        if dz in BOTH or dc == 0:
            found.append((dx, dy, dc))
    return sorted(found, key=lambda t: -min(t[0], NX - t[0]) - min(t[1], NY - t[1]))


def peers():
    found = [(dz, 0, dy, 0) for dz in range(1, NZ) for dy in range(NY)]
    found += [(0, *at) for at in offsets(BOTH[0])] + [(dz, 0, 0, 1) for dz in WHOLE]

    def hops(t):
        return min(t[0], NZ - t[0]) + min(t[1], NX - t[1]) + min(t[2], NY - t[2])

    return sorted(found, key=lambda t: -hops(t))


PEERS = peers()
NEXT = 16


def bounds(len_ref, row):
    along = len_ref[pl.ds(row, 1), :].astype(F32)
    k = lax.broadcasted_iota(jnp.int32, (DOCS_ROW, DOCS_ROW), 0)
    l = lax.broadcasted_iota(jnp.int32, (DOCS_ROW, DOCS_ROW), 1)
    spread = jnp.broadcast_to(along, (DOCS_ROW, DOCS_ROW))
    down = jnp.sum(jnp.where(k == l, spread, 0.0), axis=1, keepdims=True)
    finish_down = jnp.sum(jnp.where(l <= k, spread, 0.0), axis=1, keepdims=True)
    start_down = finish_down - down
    start_along = jnp.sum(jnp.where(k < l, jnp.broadcast_to(down, (DOCS_ROW, DOCS_ROW)), 0.0), axis=0, keepdims=True)
    return down, start_down, finish_down, start_along


def split(value):
    high = value.astype(BF16)
    return high, (value - high.astype(F32)).astype(BF16)


def nt_dot(a, b):
    return lax.dot_general(a, b, (((1,), (1,)), ((), ())), preferred_element_type=F32)


def pool_kernel(
    h_hbm, len_hbm, partner_hbm, w_hbm,
    hv, bb_ref, a_ref, ww_ref, loss_ref,
    len_ref, partner_ref, w_ref, sb, csend, crecv, rbuf, rs_in, pooled, u, gram, sym,
    load_sem, small_sem, core_send, core_recv, rs_send, rs_recv, z_send, z_recv, p_send, p_recv, f_send, f_recv, n_send,
):
    x = lax.axis_index("dp")
    seq = lax.axis_index("seq")
    chip = lax.div(seq, NCORE)
    core = lax.rem(seq, NCORE)
    z = lax.div(chip, NY)
    y = lax.rem(chip, NY)
    rows = (1 - core, core)

    def device(to_x, to_chip, to_core=core):
        return (to_x, to_chip * NCORE + to_core)

    def offset(dx, dz, dy, dc=None):
        return device(
            lax.rem(x + dx, NX),
            lax.rem(z + dz, NZ) * NY + lax.rem(y + dy, NY),
            lax.rem(core + dc, NCORE) if dc is not None else core,
        )

    other_core = (x, chip * NCORE + 1 - core)

    barrier = pltpu.get_barrier_semaphore()

    def greet(to):
        pl.semaphore_signal(barrier, inc=1, device_id=to, device_id_type=MESH)

    for dz, dx, dy, dc in PEERS[:NEXT]:
        greet(offset(dx, dz, dy, dc))

    small = []
    for n, (here, there) in enumerate(
        ((len_hbm, len_ref), (w_hbm, w_ref), (partner_hbm, partner_ref))
    ):
        copy = pltpu.make_async_copy(here, there, small_sem.at[n])
        copy.start()
        small.append(copy)
    loads = []
    for o in range(2):
        for q in range(PARTS):
            part = pl.ds(q * (TOK // PARTS), TOK // PARTS)
            copy = pltpu.make_async_copy(
                h_hbm.at[rows[o], part], hv.at[rows[o], part], load_sem.at[o * PARTS + q]
            )
            loads.append(copy)
    for copy in loads[:IN_FLIGHT]:
        copy.start()

    for dz, dx, dy, dc in PEERS[NEXT:]:
        greet(offset(dx, dz, dy, dc))

    def squares(o, q):
        n = o * PARTS + q
        loads[n].wait()
        if n + IN_FLIGHT < len(loads):
            loads[n + IN_FLIGHT].start()
        at = pl.ds(q * (TOK // PARTS), TOK // PARTS)
        acc = jnp.zeros((TOK // PARTS, 128), F32)
        for t in range(D // 128):
            v = hv[rows[o], at, t * 128 : (t + 1) * 128].astype(F32)
            acc = acc + v * v
        sb[o, at, :] = acc

    along = (seq * TOK + lax.broadcasted_iota(jnp.int32, (DOCS_ROW, TOK), 1)).astype(F32)

    def selector(o):
        _, start_down, finish_down, _ = bounds(len_ref, rows[o])
        inv = lax.rsqrt(jnp.sum(sb[o].T, axis=0, keepdims=True) * (1.0 / D) + EPS)
        member = (along >= start_down) & (along < finish_down)
        high, low = split(jnp.where(member, inv, 0.0))
        return jnp.concatenate([high, low], axis=0)

    def sums(chosen, o, part):
        columns = pl.ds(pl.multiple_of(part * (D // PARTS), D // PARTS), D // PARTS)
        both = jnp.dot(chosen, hv[rows[o], :, columns], preferred_element_type=F32)
        return both[0:DOCS_ROW] + both[DOCS_ROW : 2 * DOCS_ROW]

    per_part = CHIPS // PARTS
    order = [lax.rem(lax.div(z * PARTS, NZ) + n, PARTS) for n in (2, 1, 3, 0)]
    for q in range(PARTS):
        squares(0, q)
    for copy in small:
        copy.wait()
    chosen = selector(0)
    for part in order:
        value = sums(chosen, 0, part)
        for b in range(per_part):
            csend[part * per_part + b] = value[:, b * LANES : (b + 1) * LANES]
    for q in range(PARTS):
        squares(1, q)
    chosen = selector(1)
    for part in order:
        value = sums(chosen, 1, part)
        for b in range(per_part):
            rbuf[part * per_part + b] = value[:, b * LANES : (b + 1) * LANES]
    pl.semaphore_wait(barrier, len(PEERS))
    core_copies = []
    for q, part in enumerate(order):
        at = pl.ds(part * per_part, per_part)
        copy = pltpu.make_async_remote_copy(
            csend.at[at], crecv.at[at], core_send.at[q], core_recv.at[q],
            device_id=other_core, device_id_type=MESH,
        )
        copy.start()
        core_copies.append(copy)
    for q, part in enumerate(order):
        core_copies[q].wait_recv()
        at = pl.ds(part * per_part, per_part)
        rbuf[at] = rbuf[at] + crecv[at]
        for b in range(per_part):
            along_y = lax.rem(y + (2, 1, 3, 0)[b // (NZ // PARTS)], NY)
            to = part * per_part + b % (NZ // PARTS) * NY + along_y

            def scatter(to=to):
                pltpu.make_async_remote_copy(
                    rbuf.at[to], rs_in.at[chip], rs_send, rs_recv,
                    device_id=device(x, to), device_id_type=MESH,
                ).start()

            if q + 1 < PARTS:
                scatter()
            else:
                pl.when(to != chip)(scatter)
    for copy in core_copies:
        copy.wait_send()

    rs_in[pl.ds(chip, 1)] = rbuf[pl.ds(chip, 1)]
    for o in range(2):
        square = jnp.sum(sb[o], axis=1, keepdims=True) * (1.0 / D)
        sb[o] = jnp.broadcast_to(lax.rsqrt(square + EPS), (TOK, 128))
    u[...] = jnp.zeros_like(u)
    gram[...] = jnp.zeros_like(gram)
    lengths, _, _, _ = bounds(len_ref, core)
    pltpu.make_async_remote_copy(
        rbuf.at[pl.ds(0, CHIPS - 1)], rs_in.at[pl.ds(0, CHIPS - 1)], rs_send, rs_recv,
        device_id=other_core, device_id_type=MESH,
    ).wait()
    total = jnp.sum(rs_in[...], axis=0)
    gain = w_ref[:, pl.ds(pl.multiple_of(chip * LANES, LANES), LANES)]
    pooled[chip, x, core] = total * gain / lengths

    mine = pooled.at[chip, x, core]

    def passed(dz):
        return pooled.at[lax.rem(z + NZ - dz, NZ) * NY + y, x, core]

    def send(tile, dz, to):
        pltpu.make_async_remote_copy(
            tile, tile, p_send, p_recv.at[dz], device_id=to, device_id_type=MESH
        ).start()

    def to_plane(dz):
        tile = passed(dz)
        for dx, dy, dc in offsets(dz):
            send(tile, dz, offset(dx, 0, dy, dc))

    for dz in RELAYED[::-1]:
        pltpu.make_async_remote_copy(
            mine, mine, z_send, z_recv.at[dz], device_id=offset(0, dz, 0), device_id_type=MESH
        ).start()
    to_plane(0)
    for dz in RELAYED:
        tile = passed(dz)
        pltpu.make_async_remote_copy(
            tile, tile, z_send, z_recv.at[dz], device_id=other_core, device_id_type=MESH
        ).wait_recv()
        to_plane(dz)

    def take(dz):
        parts = PLANE * NCORE if dz in WHOLE else PLANE * NCORE - 1 if dz in BOTH else PLANE - 1
        got = pl.ds(0, parts)
        pltpu.make_async_remote_copy(
            rs_in.at[got], rs_in.at[got], p_send, p_recv.at[dz],
            device_id=other_core, device_id_type=MESH,
        ).wait_recv()
        if dz in BOTH or dz in WHOLE:
            return None
        at = pl.ds(lax.rem(z + NZ - dz, NZ) * NY, NY)
        copy = pltpu.make_async_remote_copy(
            pooled.at[at, :, core], pooled.at[at, :, core], f_send.at[dz], f_recv.at[dz],
            device_id=other_core, device_id_type=MESH,
        )
        if dz == 0:
            for to in WHOLE:
                for dc in range(NCORE):
                    pltpu.make_async_remote_copy(
                        pooled.at[at, :, core], pooled.at[at, :, core], n_send, p_recv.at[to],
                        device_id=offset(0, to, 0, dc), device_id_type=MESH,
                    ).start()
        copy.start()
        return copy

    def products(dz, last=False):
        plane = lax.rem(z + NZ - dz, NZ)
        columns = pl.ds(pl.multiple_of(plane * ZCOLS, ZCOLS), ZCOLS)
        value = jnp.concatenate(
            [pooled[plane * NY + i].reshape(NDOC, LANES) for i in range(NY)], axis=1
        )
        high, low = split(value)
        gram[...] += nt_dot(
            jnp.concatenate([high, high, low], axis=1), jnp.concatenate([high, low, high], axis=1)
        )
        high, low = split(value * w_ref[:, columns])
        both = jnp.concatenate([high, low], axis=0)

        def inner():
            ww_ref[:, columns] = both
            for o in range(2):
                u[o] += nt_dot(hv[rows[o], :, columns], both)

        if last:
            return inner
        inner()

    held = []
    for dz in TAKEN:
        copy = take(dz)
        if copy is not None:
            held.append((dz, copy))
            if len(held) < 2:
                continue
        while len(held) > (copy is not None):
            first, given = held.pop(0)
            given.wait()
            products(first)
        if copy is None:
            rest = products(dz, dz == TAKEN[-1])

    k = lax.broadcasted_iota(jnp.int32, (NDOC, NDOC), 0)
    l = lax.broadcasted_iota(jnp.int32, (NDOC, NDOC), 1)
    eye = k == l
    table = gram[...]
    only = jnp.where(eye, table, 0.0)
    norm2 = jnp.sum(only, axis=1, keepdims=True) + EPS
    norms = jnp.sqrt(norm2) * jnp.sqrt(jnp.sum(only, axis=0, keepdims=True) + EPS)
    scaled = 1.0 / (norms * SHARPNESS)
    logits = table * scaled
    weights = jnp.where(eye, 0.0, jnp.exp(logits))
    sum_down = jnp.sum(weights, axis=1, keepdims=True)
    sum_along = jnp.sum(weights, axis=0, keepdims=True)
    pair = jnp.where(partner_ref[...] == k, 1.0, 0.0)
    target = jnp.sum(jnp.sum(pair * logits, axis=1, keepdims=True), axis=0, keepdims=True)
    logs = jnp.sum(jnp.log(sum_down), axis=0, keepdims=True)
    loss_ref[...] = (logs - target) * (1.0 / NDOC)
    change = (weights * (1.0 / sum_down + 1.0 / sum_along) - 2.0 * pair) * (1.0 / NDOC)
    own = jnp.sum(change * logits, axis=1, keepdims=True) / norm2
    sym[...] = change * scaled - jnp.where(eye, own, 0.0)

    rest()

    place = (seq * TOK + lax.broadcasted_iota(jnp.int32, (TOK, 128), 0)).astype(F32)
    for o in range(2):
        lengths, _, _, start_along = bounds(len_ref, rows[o])
        ours = sym[pl.ds(pl.multiple_of((x * NCORE + rows[o]) * DOCS_ROW, DOCS_ROW), DOCS_ROW), :]
        ours = ours * (LOSS_SCALE / lengths)
        ours = jnp.concatenate([ours, ours], axis=1)
        mix = jnp.broadcast_to(ours[0:1], (TOK, 128))
        for d in range(1, DOCS_ROW):
            mix = jnp.where(place >= start_along[:, d : d + 1], ours[d : d + 1], mix)
        inner = jnp.sum(u[o] * mix, axis=1, keepdims=True) * (1.0 / D)
        inv = sb[o]
        a_ref[rows[o]] = inv * inv * inv * inner
        high, low = split(inv * mix)
        bb_ref[rows[o], :, 0:128] = high
        bb_ref[rows[o], :, 128:256] = low

    some = pl.ds(0, len(RELAYED))
    pltpu.make_async_copy(rs_in.at[some], rs_in.at[some], z_send).wait()
    for _ in range(2 * len(WHOLE)):
        some = pl.ds(0, PLANE)
        pltpu.make_async_copy(rs_in.at[some], rs_in.at[some], n_send).wait()
    left = sum(len(offsets(dz)) for dz in (0, *RELAYED))
    while left:
        some = pl.ds(0, min(left, CHIPS))
        pltpu.make_async_copy(rs_in.at[some], rs_in.at[some], p_send).wait()
        left -= min(left, CHIPS)


def grad_kernel(h_ref, bb_ref, a_ref, ww_ref, loss_ref, out_hbm, loss_out, out, sem):
    copies = [pltpu.make_async_copy(loss_ref, loss_out, sem.at[len(WIDTHS)])]
    copies[0].start()
    for n, width in enumerate(WIDTHS):
        columns = slice(sum(WIDTHS[:n]), sum(WIDTHS[: n + 1]))
        both = ww_ref[:, columns]
        both = jnp.concatenate([both, both], axis=0)
        for r in range(2):
            first = jnp.dot(bb_ref[r], both, preferred_element_type=F32)
            a = jnp.concatenate([a_ref[r]] * (width // 128), axis=1)
            out[r, :, columns] = (first - h_ref[r, :, columns].astype(F32) * a).astype(BF16)
        copy = pltpu.make_async_copy(out.at[:, :, columns], out_hbm.at[:, :, columns], sem.at[n])
        copy.start()
        copies.append(copy)
    for copy in copies:
        copy.wait()


def shards(hidden, doc_lengths, partner, closing_layer_weight):
    vmem = pl.BlockSpec(memory_space=pltpu.VMEM)
    hbm = pl.BlockSpec(memory_space=pltpu.HBM)
    dma = pltpu.SemaphoreType.DMA
    arguments = (hidden, doc_lengths, partner.reshape(1, NDOC), closing_layer_weight.reshape(1, D))
    h, bb, a, ww, loss = pl.pallas_call(
        pool_kernel,
        out_shape=(
            pltpu.VMEM((2, TOK, D), BF16),
            pltpu.VMEM((2, TOK, 256), BF16),
            pltpu.VMEM((2, TOK, 128), F32),
            pltpu.VMEM((2 * NDOC, D), BF16),
            pltpu.VMEM((1, 1), F32),
        ),
        in_specs=[hbm] * 4,
        out_specs=(vmem,) * 5,
        scratch_shapes=[
            pltpu.VMEM((2, DOCS_ROW), jnp.int32),
            pltpu.VMEM((1, NDOC), jnp.int32),
            pltpu.VMEM((1, D), F32),
            pltpu.VMEM((2, TOK, 128), F32),
            pltpu.VMEM((CHIPS, DOCS_ROW, LANES), F32),
            pltpu.VMEM((CHIPS, DOCS_ROW, LANES), F32),
            pltpu.VMEM((CHIPS, DOCS_ROW, LANES), F32),
            pltpu.VMEM((CHIPS, DOCS_ROW, LANES), F32),
            pltpu.VMEM((CHIPS, NX, NCORE, DOCS_ROW, LANES), F32),
            pltpu.VMEM((2, TOK, 128), F32),
            pltpu.VMEM((NDOC, NDOC), F32),
            pltpu.VMEM((NDOC, NDOC), F32),
            dma((2 * PARTS,)), dma((3,)),
            dma((PARTS,)), dma((PARTS,)),
            dma, dma,
            dma, dma((NZ,)),
            dma, dma((NZ,)),
            dma((NZ,)), dma((NZ,)),
            dma,
        ],
        compiler_params=pltpu.CompilerParams(
            collective_id=0, has_side_effects=True, vmem_limit_bytes=16 * 1024 * 1024
        ),
        name="pool_and_loss",
    )(*(pltpu.with_memory_space_constraint(v, pltpu.HBM) for v in arguments))
    out, loss = pl.pallas_call(
        grad_kernel,
        out_shape=(
            jax.ShapeDtypeStruct((2, TOK, D), BF16),
            jax.ShapeDtypeStruct((1, 1), F32),
        ),
        in_specs=[vmem] * 5,
        out_specs=(pl.BlockSpec(memory_space=pl.ANY),) * 2,
        scratch_shapes=[pltpu.VMEM((2, TOK, D), BF16), dma((len(WIDTHS) + 1,))],
        compiler_params=pltpu.CompilerParams(vmem_limit_bytes=16 * 1024 * 1024),
        name="hidden_gradient",
    )(h, bb, a, ww, loss)
    return out, loss.reshape(())


def solution(mesh):
    in_specs = (P("dp", "seq", None), P("dp", None), P(), P())
    out_specs = (P("dp", "seq", None), P())
    return jax.shard_map(shards, mesh=mesh, in_specs=in_specs, out_specs=out_specs, check_vma=False)
```
